256 devices in a mesh: dp: 16 (over y, x_hi, core), expert: 16 (over x_lo, z).
Axes of the slice: x: 4 (x_hi: 2, x_lo: 2; x = x_hi * 2 + x_lo), y: 4, z: 8, core: 2. Of those that a mesh axis runs over, the one named last changes fastest.
Arguments:
- tokens: bfloat16 [2048, 3584], P('expert', 'dp'), may hold values from -6 to 6
- routes: int32 [2048, 8], replicated, may hold values from 0 to 47, all different within a row; in each aligned block of 2048 rows (0 to 2047, 2048 to 4095, ...) at most 362 rows name the same one
- combine: float32 [2048, 8], replicated, may hold values from 0.02 to 0.5
- w_gate: bfloat16 [48, 3584, 1280], P('expert', 'dp'), may hold values from -0.09375 to 0.09375
- w_up: bfloat16 [48, 3584, 1280], P('expert', 'dp'), may hold values from -0.09375 to 0.09375
- w_down: bfloat16 [48, 1280, 3584], P('expert', None, 'dp'), may hold values from -0.15625 to 0.15625
- cotangent: bfloat16 [2048, 3584], P('expert', 'dp'), may hold values from -6 to 6
Outputs:
- mixed: bfloat16 [2048, 3584], P('expert', 'dp')
- grad_tokens: bfloat16 [2048, 3584], P('expert', 'dp')
- grad_gate: bfloat16 [48, 3584, 1280], P('expert', 'dp')
- grad_up: bfloat16 [48, 3584, 1280], P('expert', 'dp')
- grad_down: bfloat16 [48, 1280, 3584], P('expert', None, 'dp')
The draws below stay inside these ranges and needn't reach their ends.
Inputs may be any that keep to these rules, and one draw needn't show every extreme that they name: `routes`: each token names 8 different experts; no expert is named by more than 362 tokens, a bound that some block reaches.
All inputs are finite; a program needn't handle non-finite values.
Results may differ from the reference program's by a relative error of at most 0.03.
Values may be sent and summed in bfloat16 or wider, within the bound.
A program may use at most 128 MiB of HBM per device.

```python
import math
import jax
import jax.numpy as jnp
import numpy as np
from jax import lax

D = 3584
FF = 1280
TOPK = 8
EXPERTS = 48
TOKENS = 2048
CAP = 362
N_DP = 16


def block_levels(stream_key, dims, shards, smallest, high):
    def one(dim, shards_of):
        draws = jax.random.uniform(jax.random.fold_in(jax.random.fold_in(stream_key, 6), dim), (shards_of,), jnp.float32, smallest / len(shards), high / len(shards))
        return jnp.repeat(jnp.exp(draws), dims[dim] // shards_of).reshape((-1,) + (1,) * (len(dims) - dim - 1))

    loudness = one(*shards[0])
    for cut in shards[1:]:
        loudness = loudness * one(*cut)
    return loudness


def deal_out(rng, own, number, rows, amount, top, most, slope):
    sequence = jax.random.permutation(rng, amount)
    packed, usual = shares(amount, rows * top, most, slope, True), shares(amount, rows * top, most, slope, False)
    places = jnp.arange(amount)

    def named(sizes, rotation):
        used = int((sizes > 0).sum())
        fixed = max(1, used // 4)
        moved = fixed + (places - fixed + rotation * (used - fixed)) % max(1, amount - fixed)
        return jnp.zeros((amount,), jnp.int32).at[sequence[jnp.where(places < fixed, places, moved)]].set(jnp.asarray(sizes, jnp.int32))

    sizes = jnp.where(number % 4 == 0, named(packed, number // 4), named(usual, number - number // 4 - 1))
    mixed = jax.random.permutation(jax.random.fold_in(own, 3), amount)
    donor, sink = mixed[0:amount // 2 * 2:2], mixed[1:amount // 2 * 2:2]
    room = jnp.minimum(sizes[donor] - 1, most - sizes[sink]) // 2
    room = jnp.where((donor == sequence[0]) | (sink == sequence[0]) | (sizes[sink] == 0), 0, jnp.maximum(room, 0))
    moved = jax.random.randint(jax.random.fold_in(own, 4), (amount // 2,), 0, 1 << 20) % (room + 1)
    sizes = sizes.at[donor].add(-moved).at[sink].add(moved)
    labels = jnp.searchsorted(jnp.cumsum(sizes), jnp.arange(rows * top), side="right").astype(jnp.int32)
    grid = labels.reshape(top, rows).T
    grid = grid[jax.random.permutation(jax.random.fold_in(own, 1), rows)]
    rotation = jax.random.randint(jax.random.fold_in(own, 2), (rows, 1), 0, top)
    return jnp.take_along_axis(grid, (jnp.arange(top)[None, :] + rotation) % top, axis=1)


def shares(amount, total, limit, slope, full):
    portions = [(1 << 20) // math.isqrt(grade ** slope) + 1 for grade in range(1, amount + 1)]
    largest = limit if full else min(limit, max(-(-total // amount), total * portions[0] // sum(portions)))
    least = 1 if total - largest >= amount - 1 else 0
    counts, spare = [largest] + [least] * (amount - 1), total - largest - least * (amount - 1)
    while spare > 0:
        free = [i for i in range(1, amount) if counts[i] < largest] or [i for i in range(1, amount) if counts[i] < limit]
        pool, left = sum([portions[i] for i in free]), spare
        for i in free:
            extra = min(limit - counts[i], max(1, left * portions[i] // pool), spare)
            counts[i] = counts[i] + extra
            spare = spare - extra
    return np.array(counts)


def centred(key, extent, deviation, limit, split=(), held_as=jnp.bfloat16):
    entries = jax.random.normal(key, extent, jnp.float32) * deviation
    if len(split) > 0:
        entries = block_levels(key, extent, split, -0.22, 0.18) * entries
    return jnp.clip(entries, min=-limit, max=limit).astype(held_as)


def setup_inputs(seed: int = 0) -> dict:
    streams_of = jax.random.split(jax.random.key(seed), 8)
    tokens = centred(streams_of[0], (TOKENS, D), 1.0, 6.0, ((0, 16), (1, 16)))
    routes_keys = jax.random.split(jax.random.fold_in(streams_of[1], 1), TOKENS // TOKENS)
    routes_turns = jax.random.permutation(jax.random.fold_in(streams_of[1], 3), TOKENS // TOKENS)
    routes = jax.vmap(lambda own, number: deal_out(jax.random.fold_in(streams_of[1], 2), own, number, TOKENS, EXPERTS, TOPK, CAP, 2))(routes_keys, routes_turns).reshape((TOKENS, TOPK))
    combine = jnp.clip(jnp.exp(jax.random.uniform(streams_of[2], (TOKENS, TOPK), jnp.float32, math.log(0.02), math.log(0.5))), 0.02, 0.5)
    w_gate = centred(streams_of[3], (EXPERTS, D, FF), D ** -0.5, 0.09375, ((0, 16), (1, 16)))
    w_up = centred(streams_of[4], (EXPERTS, D, FF), D ** -0.5, 0.09375, ((0, 16), (1, 16)))
    w_down = centred(streams_of[5], (EXPERTS, FF, D), FF ** -0.5, 0.15625, ((0, 16), (2, 16)))
    cotangent = centred(streams_of[6], (TOKENS, D), 1.0, 6.0, ((0, 16), (1, 16)))
    return {"tokens": tokens, "routes": routes, "combine": combine, "w_gate": w_gate, "w_up": w_up, "w_down": w_down, "cotangent": cotangent}


def build_slots(routes, combine, experts, capacity):
    tok_count = routes.shape[0]
    local_ids = jnp.arange(experts, dtype=jnp.int32)
    matched = routes[:, :, None] == local_ids[None, None, :]
    routed = jnp.any(matched, axis=1)
    weight = jnp.sum(jnp.where(matched, combine[:, :, None], jnp.zeros_like(combine)[:, :, None]), axis=1)
    ranked = jnp.cumsum(routed.astype(jnp.int32), axis=0) - 1
    slot_pos = jnp.where(routed, ranked, capacity).astype(jnp.int32)
    column = jnp.broadcast_to(local_ids[None, :], slot_pos.shape)
    row_ids = jnp.broadcast_to(jnp.arange(tok_count, dtype=jnp.int32)[:, None], slot_pos.shape)
    tok_index = jnp.zeros((experts, capacity + 1), jnp.int32).at[column, slot_pos].set(row_ids)[:, :capacity]
    slot_weight = jnp.zeros((experts, capacity + 1), jnp.float32).at[column, slot_pos].set(weight.astype(jnp.float32))[:, :capacity]
    slot_live = jnp.zeros((experts, capacity + 1), jnp.float32).at[column, slot_pos].set(routed.astype(jnp.float32))[:, :capacity]
    return tok_index, slot_weight, slot_live


def block_sum(left_parts, right_parts, form, shape):
    def step(total, pair):
        term = jnp.einsum(form, pair[0].astype(jnp.float32), pair[1].astype(jnp.float32))
        rounded = lax.optimization_barrier(term.astype(jnp.bfloat16))
        return total + rounded.astype(jnp.float32), None

    total, unused = lax.scan(step, jnp.zeros(shape, jnp.float32), (left_parts, right_parts))
    return total


def reference(tokens, routes, combine, w_gate, w_up, w_down, cotangent):
    width_block = D // N_DP
    tok_index, slot_weight, slot_live = build_slots(routes, combine, EXPERTS, CAP)
    picked = tokens[tok_index] * slot_live[:, :, None].astype(jnp.bfloat16)
    left_parts = jnp.moveaxis(picked.reshape(EXPERTS, CAP, N_DP, width_block), 2, 0)
    gate_parts = jnp.moveaxis(w_gate.reshape(EXPERTS, N_DP, width_block, FF), 1, 0)
    up_parts = jnp.moveaxis(w_up.reshape(EXPERTS, N_DP, width_block, FF), 1, 0)
    shape = (EXPERTS, CAP, FF)
    gate = block_sum(left_parts, gate_parts, "ecd,edf->ecf", shape)
    up = block_sum(left_parts, up_parts, "ecd,edf->ecf", shape)
    sig_gate = jax.nn.sigmoid(gate)
    hidden = (gate * sig_gate * up).astype(jnp.bfloat16)
    slot_out = jnp.einsum("ecf,efd->ecd", hidden.astype(jnp.float32), w_down.astype(jnp.float32))
    mixed = jnp.zeros((TOKENS, D), jnp.float32).at[tok_index].add(slot_out * slot_weight[:, :, None]).astype(jnp.bfloat16)
    cot_slots = (cotangent[tok_index].astype(jnp.float32) * slot_weight[:, :, None]).astype(jnp.bfloat16)
    grad_down = jnp.einsum("ecf,ecd->efd", hidden.astype(jnp.float32), cot_slots.astype(jnp.float32)).astype(jnp.bfloat16)
    cot_parts = jnp.moveaxis(cot_slots.reshape(EXPERTS, CAP, N_DP, width_block), 2, 0)
    down_parts = jnp.moveaxis(w_down.reshape(EXPERTS, FF, N_DP, width_block), 2, 0)
    back = block_sum(cot_parts, down_parts, "ecd,efd->ecf", shape)
    gate_grad = (back * up * sig_gate * (1.0 + gate * (1.0 - sig_gate))).astype(jnp.bfloat16)
    up_grad = (back * gate * sig_gate).astype(jnp.bfloat16)
    picked_wide = picked.astype(jnp.float32)
    grad_gate = jnp.einsum("ecd,ecf->edf", picked_wide, gate_grad.astype(jnp.float32)).astype(jnp.bfloat16)
    grad_up = jnp.einsum("ecd,ecf->edf", picked_wide, up_grad.astype(jnp.float32)).astype(jnp.bfloat16)
    input_slot = jnp.einsum("ecf,edf->ecd", gate_grad.astype(jnp.float32), w_gate.astype(jnp.float32))
    input_slot = input_slot + jnp.einsum("ecf,edf->ecd", up_grad.astype(jnp.float32), w_up.astype(jnp.float32))
    grad_tokens = jnp.zeros((TOKENS, D), jnp.float32).at[tok_index].add(input_slot).astype(jnp.bfloat16)
    return (mixed, grad_tokens, grad_gate, grad_up, grad_down)
```

```python
import functools

import jax
import jax.numpy as jnp
from jax import lax
from jax.experimental import pallas as pl
from jax.experimental.pallas import tpu as pltpu
from jax.sharding import PartitionSpec as P

MESH = pl.DeviceIdType.MESH
BF = jnp.bfloat16
F32 = jnp.float32

SK = 2
CP = 384
ROWS = 48
WA = 384
WB = 128


def dot(a, b):
    return jnp.dot(a, b, preferred_element_type=F32)


def dot_nt(a, b):
    return lax.dot_general(a, b, (((1,), (1,)), ((), ())), preferred_element_type=F32)


def dot_tn(a, b):
    return lax.dot_general(a, b, (((0,), (0,)), ((), ())), preferred_element_type=F32)


def kernel(
    tok, cot, routes, combine, wg, wu, wd,
    mixed_out, gt_out, gg_out, gu_out, gd_out,
    W, WD, TK, A, WT, PK, PT, PSa, PSb, Qa, Qb, CRa, CRb,
    Y1a, Y2a, Xa, XSa, Xb, Y1b, Y2b, GUa, GUb, Fa, Fb,
    YT, MP, MR, MX, MXS, GGs, GUs, GDs, TP, TPB,
    wsem, osem, rs_s, rs_r, ag_s, ag_r, tk_s, tk_r, m_s, m_r,
):
    experts, width = wg.shape[0], wg.shape[1]
    half = wg.shape[2] // 2
    tokens = routes.shape[1]
    d = lax.axis_index("dp")
    ex = lax.axis_index("expert")
    y, xh, c = d // 4, (d // 2) % 2, d % 2
    xl, z = ex // 8, ex % 8
    yr, yl, yo = (y + 1) % 4, (y + 3) % 4, (y + 2) % 4
    xo, co, xlo = 1 - xh, 1 - c, 1 - xl

    def dev(yy, xx, cc, ll, zz):
        return (yy * 4 + xx * 2 + cc, ll * 8 + zz)

    CORE = dev(y, xh, co, xl, z)
    YR = dev(yr, xh, c, xl, z)
    YL = dev(yl, xh, c, xl, z)
    XH = dev(y, xo, c, xl, z)
    XL = dev(y, xh, c, xlo, z)
    ZR = dev(y, xh, c, xl, (z + 1) % 8)
    ZL = dev(y, xh, c, xl, (z + 7) % 8)

    def remote(src, dst, ss, rr, to):
        return pltpu.make_async_remote_copy(
            src_ref=src, dst_ref=dst, send_sem=ss, recv_sem=rr,
            device_id=to, device_id_type=MESH,
        )

    def weight_copies():
        out = []
        for i, w in enumerate((wg, wu)):
            for h in range(2):
                out.append(pltpu.make_async_copy(
                    w.at[:, :, pl.ds(h * half, half)], W.at[i, h], wsem.at[i * 2 + h]))
        for h in range(2):
            out.append(pltpu.make_async_copy(
                wd.at[:, pl.ds(h * half, half), :], WD.at[h], wsem.at[4 + h]))
        return out

    barrier = pltpu.get_barrier_semaphore()
    for peer in (CORE, YR, YL, XH, XL, ZR, ZL):
        pl.semaphore_signal(barrier, inc=1, device_id=peer, device_id_type=MESH)
    for cp in weight_copies():
        cp.start()

    TPB[...] = jnp.zeros_like(TPB)
    for i, src in enumerate((tok, cot)):
        TPB[:, :width] = src[...].astype(F32)
        TK[i, xl, z] = jnp.transpose(TPB[...])[:width].astype(BF)
    pl.semaphore_wait(barrier, 7)

    def tk_x(i):
        r = TK.at[i, xl, z]
        return remote(r, r, tk_s.at[i, 16], tk_r.at[i, 16], XL)

    def tk_z(i, way, s, b):
        zs = (z + 8 - (s - 1)) % 8 if way == 0 else (z + (s - 1)) % 8
        r = TK.at[i, b, zs]
        n = way * 8 + (s - 1) * 2 + b
        return remote(r, r, tk_s.at[i, n], tk_r.at[i, n], ZR if way == 0 else ZL)

    def tk0(i):
        tk_z(i, 0, 1, xl).start()
        tk_z(i, 1, 1, xl).start()
        tk_x(i).start()

    def tk1(i):
        tk_x(i).wait_recv()
        tk_z(i, 0, 1, xlo).start()
        tk_z(i, 1, 1, xlo).start()

    def tk_hop(i, s):
        if s < 3:
            for b in (xl, xlo):
                for way in (0, 1):
                    tk_z(i, way, s, b).wait_recv()
                    tk_z(i, way, s + 1, b).start()
        elif s == 3:
            for way in (0, 1):
                tk_z(i, way, 3, way).wait_recv()
                tk_z(i, way, 4, way).start()
            for way in (0, 1):
                tk_z(i, way, 3, 1 - way).wait_recv()
        else:
            for way in (0, 1):
                tk_z(i, way, 4, way).wait_recv()

    def tk_drain(i):
        tk_x(i).wait_send()
        for way in (0, 1):
            for s in (1, 2, 3):
                for b in (0, 1):
                    tk_z(i, way, s, b).wait_send()
            tk_z(i, way, 4, way).wait_send()

    def token_rows(i):
        return jnp.concatenate([TK[i, n // 8, n % 8] for n in range(16)], axis=1)

    def m_z(i, way, s):
        zd = (z + 5 - s) % 8 if way == 0 else (z + 3 + s) % 8
        n = way * 4 + s - 1
        to = ZR if way == 0 else ZL
        if s == 1:
            return remote(MP.at[i, way, zd], MR.at[i, way, 0, way], m_s.at[i, n], m_r.at[i, n], to)
        return remote(MP.at[i, :, zd], MR.at[i, way, s - 1], m_s.at[i, n], m_r.at[i, n], to)

    def m_x(i):
        return remote(MXS.at[i], MX.at[i], m_s.at[i, 8], m_r.at[i, 8], XL)

    def m_partial(i):
        for q in range(4):
            acc = dot(YT[i, 0], A[0, :, q * 512:(q + 1) * 512])
            for e in range(1, experts):
                acc = acc + dot(YT[i, e], A[e, :, q * 512:(q + 1) * 512])
            acc = acc.astype(BF)
            for j in range(4):
                n = q * 4 + j
                MP[i, n // 8, n % 8] = acc[:, j * 128:(j + 1) * 128]
        m_z(i, 0, 1).start()
        m_z(i, 1, 1).start()

    def m_step(i, s):
        for way in (0, 1):
            zd = (z + 5 - s) % 8 if way == 0 else (z + 3 + s) % 8
            m_z(i, way, s - 1).wait_recv()
            if s == 2:
                MP[i, way, zd] = (MP[i, way, zd].astype(F32) + MR[i, way, 0, way].astype(F32)).astype(BF)
            else:
                for b in (0, 1):
                    MP[i, b, zd] = (MP[i, b, zd].astype(F32) + MR[i, way, s - 2, b].astype(F32)).astype(BF)
            m_z(i, way, s).start()

    def m_sum(i, b):
        return MP[i, b, z].astype(F32) + MR[i, 0, 3, b].astype(F32) + MR[i, 1, 3, b].astype(F32)

    def m_end(i):
        m_z(i, 0, 4).wait_recv()
        m_z(i, 1, 4).wait_recv()
        MXS[i] = m_sum(i, xlo).astype(BF)
        m_x(i).start()

    def m_final(i, out):
        m_x(i).wait_recv()
        TP[0:width, 0:128] = m_sum(i, xl) + MX[i].astype(F32)
        out[...] = jnp.transpose(TP[0:256, 0:128])[:, :width].astype(BF)

    def m_drain(i):
        for way in (0, 1):
            for s in (1, 2, 3, 4):
                m_z(i, way, s).wait_send()
        m_x(i).wait_send()

    def rs(k, n):
        s, r = rs_s.at[k, n], rs_r.at[k, n]
        if n == 0:
            return remote(PSa.at[k], CRa.at[k], s, r, CORE)
        if n == 1:
            return remote(PSb.at[k], CRb.at[k], s, r, CORE)
        if n == 2:
            return remote(Qa.at[k, yo, 0], Y1a.at[k, 0], s, r, YR)
        if n == 3:
            return remote(Qa.at[k, yo, 1], Y1a.at[k, 1], s, r, YL)
        if n == 4:
            return remote(Qa.at[k, yr], Y2a.at[k, 0], s, r, YR)
        if n == 5:
            return remote(Qa.at[k, yl], Y2a.at[k, 1], s, r, YL)
        if n == 6:
            return remote(XSa.at[k], Xa.at[k], s, r, XH)
        if n == 7:
            return remote(Qb.at[k, :, xo], Xb.at[k], s, r, XH)
        if n == 8:
            return remote(Qb.at[k, yo, xh, 0], Y1b.at[k, 0], s, r, YR)
        if n == 9:
            return remote(Qb.at[k, yo, xh, 1], Y1b.at[k, 1], s, r, YL)
        if n == 10:
            return remote(Qb.at[k, yr, xh], Y2b.at[k, 0], s, r, YR)
        return remote(Qb.at[k, yl, xh], Y2b.at[k, 1], s, r, YL)

    def put(ra, rb, k, v):
        v = v.astype(BF)
        ra[k] = v[:, :WA].reshape(4, 2, ROWS, WA)
        for p in range(2):
            rb[k, :, :, p] = v[:, WA + p * WB:WA + (p + 1) * WB].reshape(4, 2, ROWS, WB)

    def s0(k, part):
        put(PSa, PSb, k, part(co))
        rs(k, 0).start()
        rs(k, 1).start()
        put(Qa, Qb, k, part(c))

    def add(ref, idx, other):
        ref[idx] = (ref[idx].astype(F32) + other.astype(F32)).astype(BF)

    def s1(k):
        rs(k, 0).wait_recv()
        add(Qa, (k, yo), CRa[k, yo])
        rs(k, 2).start()
        rs(k, 3).start()
        rs(k, 1).wait_recv()
        for j in range(4):
            add(Qb, (k, j), CRb[k, j])
        rs(k, 7).start()
        for j in (yr, yl, y):
            add(Qa, (k, j), CRa[k, j])

    def s2(k):
        rs(k, 2).wait_recv()
        add(Qa, (k, yr, 0), Y1a[k, 0])
        rs(k, 4).start()
        rs(k, 3).wait_recv()
        add(Qa, (k, yl, 1), Y1a[k, 1])
        rs(k, 5).start()
        rs(k, 7).wait_recv()
        add(Qb, (k, yo, xh), Xb[k, yo])
        rs(k, 8).start()
        rs(k, 9).start()
        for j in (yr, yl, y):
            add(Qb, (k, j, xh), Xb[k, j])

    def sum_a(k, x):
        return Qa[k, y, x].astype(F32) + Y2a[k, 0, x].astype(F32) + Y2a[k, 1, x].astype(F32)

    def s3(k):
        rs(k, 8).wait_recv()
        add(Qb, (k, yr, xh, 0), Y1b[k, 0])
        rs(k, 10).start()
        rs(k, 9).wait_recv()
        add(Qb, (k, yl, xh, 1), Y1b[k, 1])
        rs(k, 11).start()
        rs(k, 4).wait_recv()
        rs(k, 5).wait_recv()
        XSa[k] = sum_a(k, xo).astype(BF)
        rs(k, 6).start()

    def s4(k):
        rs(k, 6).wait_recv()
        va = sum_a(k, xh) + Xa[k].astype(F32)
        rs(k, 10).wait_recv()
        rs(k, 11).wait_recv()
        vb = Qb[k, y, xh].astype(F32) + Y2b[k, 0].astype(F32) + Y2b[k, 1].astype(F32)
        return va, vb

    def hidden_of(gate, up):
        return (gate * jax.nn.sigmoid(gate) * up).astype(BF)

    def grads_of(back, gate, up):
        sg = jax.nn.sigmoid(gate)
        return (back * up * sg * (1.0 + gate * (1.0 - sg))).astype(BF), (back * gate * sg).astype(BF)

    def ag(g, j, n, m):
        s, r = ag_s.at[g, m], ag_r.at[g, m]
        js = pl.ds(j, n)
        if m == 0:
            ref, to = Fa.at[js, c, y, xh], XH
        elif m in (1, 2):
            ref, to = Fa.at[js, c, y, xh], (YR if m == 1 else YL)
        elif m in (3, 4):
            ref, to = Fa.at[js, c, y, xo], (YR if m == 3 else YL)
        elif m == 5:
            ref, to = Fa.at[js, c, yl, 0], YR
        elif m == 6:
            ref, to = Fa.at[js, c, yr, 1], YL
        elif m in (7, 8):
            ref, to = Fb.at[js, c, y, xh], (YR if m == 7 else YL)
        elif m == 9:
            ref, to = Fb.at[js, c, yl, xh, 0], YR
        elif m == 10:
            ref, to = Fb.at[js, c, yr, xh, 1], YL
        elif m == 11:
            ref, to = Fb.at[js, c, :, xh], XH
        elif m == 12:
            ref, to = Fa.at[js, c], CORE
        else:
            ref, to = Fb.at[js, c], CORE
        return remote(ref, ref, s, r, to)

    def ag_stage(i, g, j, n):
        if i == 0:
            for m in (0, 1, 2, 7, 8):
                ag(g, j, n, m).start()
        if i == 1:
            ag(g, j, n, 0).wait_recv()
            ag(g, j, n, 3).start()
            ag(g, j, n, 4).start()
            ag(g, j, n, 7).wait_recv()
            ag(g, j, n, 9).start()
            ag(g, j, n, 8).wait_recv()
            ag(g, j, n, 10).start()
        if i == 2:
            ag(g, j, n, 1).wait_recv()
            ag(g, j, n, 3).wait_recv()
            ag(g, j, n, 5).start()
            ag(g, j, n, 2).wait_recv()
            ag(g, j, n, 4).wait_recv()
            ag(g, j, n, 6).start()
            ag(g, j, n, 9).wait_recv()
            ag(g, j, n, 10).wait_recv()
            ag(g, j, n, 11).start()
        if i == 3:
            ag(g, j, n, 5).wait_recv()
            ag(g, j, n, 6).wait_recv()
            ag(g, j, n, 12).start()
            ag(g, j, n, 11).wait_recv()
            ag(g, j, n, 13).start()
        if i == 4:
            ag(g, j, n, 12).wait_recv()
            ag(g, j, n, 13).wait_recv()

    def full(j, h):
        return jnp.concatenate(
            [Fa[j, h].reshape(CP, WA), Fb[j, h, :, :, 0].reshape(CP, WB), Fb[j, h, :, :, 1].reshape(CP, WB)], axis=1)

    def out_copy(i, e):
        src, dst = ((GGs, gg_out), (GUs, gu_out), (GDs, gd_out))[i]
        return pltpu.make_async_copy(src.at[e], dst.at[e], osem.at[i, e])

    def turn(v):
        TP[:, :width] = v
        return jnp.transpose(TP[...])[:width].astype(BF)

    def use_hidden(e):
        acc = jnp.zeros((CP, width), F32)
        for h in range(2):
            f = full(e, h)
            acc = acc + dot(f, WD[h, e])
            GDs[e, h * half:(h + 1) * half] = dot_tn(f, PK[1, e]).astype(BF)
        out_copy(2, e).start()
        YT[0, e] = turn(acc * WT[e, :, 0:1])

    def use_grads(e):
        acc = jnp.zeros((CP, width), F32)
        for i, stage in ((0, GGs), (1, GUs)):
            for h in range(2):
                f = full(experts + 2 * e + i, h)
                acc = acc + dot_nt(f, W[i, h, e])
                stage[e, :, h * half:(h + 1) * half] = dot(PT[e], f).astype(BF)
            out_copy(i, e).start()
        YT[1, e] = turn(acc)

    tk0(0)
    TP[...] = jnp.zeros_like(TP)
    lane = lax.broadcasted_iota(jnp.int32, (1, tokens), 1)
    for e in range(experts):
        same = routes[...] == ex * experts + e
        routed = jnp.max(jnp.where(same, 1, 0), axis=0, keepdims=True)
        weight = jnp.sum(jnp.where(same, combine[...], 0.0), axis=0, keepdims=True)
        rank = jnp.broadcast_to(routed, (8, tokens))
        lanes = jnp.broadcast_to(lane, (8, tokens))
        step = 1
        while step < tokens:
            rank = rank + jnp.where(lanes >= step, pltpu.roll(rank, step, 1), 0)
            step *= 2
        pos = jnp.where(routed > 0, rank[0:1] - 1, -1)
        if e == 0:
            tk1(0)

        def fill(i, _, e=e, pos=pos, weight=weight):
            at = pl.ds(pl.multiple_of(i * 32, 32), 32)
            hit = lax.broadcasted_iota(jnp.int32, (32, tokens), 0) + i * 32 == pos
            A[e, at] = jnp.where(hit, 1.0, 0.0).astype(BF)
            WT[e, at] = jnp.broadcast_to(
                jnp.sum(jnp.where(hit, weight, 0.0), axis=1, keepdims=True), (32, 128))
            return 0

        lax.fori_loop(0, CP // 32, fill, 0)
        tk_hop(0, e + 1)
    tk_hop(0, 4)
    for cp in weight_copies():
        cp.wait()
    rows = token_rows(0)
    for e in range(experts):
        v = dot_nt(A[e], rows)
        PK[0, e] = v.astype(BF)
        PT[e] = turn(v)

    gu = 2 * experts
    items = gu + experts
    ag_h = 1 + 4 * SK
    ag_p = gu + 4 * SK
    last = ag_p + experts - 1 + 4 * SK

    def tick(t, _):
        def at(k, lo, hi, f):
            @pl.when(jnp.logical_and(k >= lo, k < hi))
            def _():
                f(k)

        def on(k, f):
            @pl.when(t == k)
            def _():
                f()

        at(t, 0, gu, lambda k: s0(k, lambda h: dot(PK[0, k // 2], W[k % 2, h, k // 2])))
        at(t, gu, items, lambda k: s0(k, lambda h: dot_nt(PK[1, k - gu], WD[h, k - gu])))
        at(t - SK, 0, items, s1)
        at(t - 2 * SK, 0, items, s2)
        at(t - 3 * SK, 0, items, s3)

        def end(k):
            va, vb = s4(k)

            @pl.when(k < gu)
            def _():
                GUa[k % 2, k // 2] = va
                GUb[k % 2, k // 2] = vb

            @pl.when(jnp.logical_and(k < gu, k % 2 == 1))
            def _():
                e = k // 2
                Fa[e, c, y, xh] = hidden_of(GUa[0, e], va)
                Fb[e, c, y, xh] = hidden_of(GUb[0, e], vb)
                ag_stage(0, e, e, 1)

            @pl.when(k >= gu)
            def _():
                e = k - gu
                j = experts + 2 * e
                Fa[j, c, y, xh], Fa[j + 1, c, y, xh] = grads_of(va, GUa[0, e], GUa[1, e])
                Fb[j, c, y, xh], Fb[j + 1, c, y, xh] = grads_of(vb, GUb[0, e], GUb[1, e])
                ag_stage(0, experts + e, j, 2)

        at(t - 4 * SK, 0, items, end)

        for i in range(1, 5):
            u = t - ag_h - i * SK

            @pl.when(jnp.logical_and(jnp.logical_and(u >= 0, u < 2 * experts), u % 2 == 0))
            def _(u=u, i=i):
                e = u // 2
                ag_stage(i, e, e, 1)
                if i == 4:
                    use_hidden(e)

            def grads_stage(e, i=i):
                ag_stage(i, experts + e, experts + 2 * e, 2)
                if i == 4:
                    use_grads(e)

            at(t - ag_p - i * SK, 0, experts, grads_stage)

        on(0, lambda: tk0(1))
        on(1, lambda: tk1(1))
        on(2, lambda: tk_hop(1, 1))
        on(3, lambda: tk_hop(1, 2))
        on(4, lambda: tk_hop(1, 3))

        def cot_slots():
            tk_hop(1, 4)
            crow = token_rows(1)
            for e in range(experts):
                PK[1, e] = (dot_nt(A[e], crow) * WT[e, :, 0:1]).astype(BF)

        on(gu - 1, cot_slots)
        m0 = ag_h + 2 * (experts - 1) + 4 * SK
        on(m0, lambda: m_partial(0))
        on(m0 + 1, lambda: m_step(0, 2))
        on(m0 + 2, lambda: m_step(0, 3))
        return 0

    lax.fori_loop(0, last + 1, tick, 0)

    m_partial(1)
    m_step(0, 4)
    m_step(1, 2)
    m_end(0)
    m_step(1, 3)
    m_final(0, mixed_out)
    m_step(1, 4)
    m_end(1)

    def drain_items(k, _):
        for n in range(12):
            rs(k, n).wait_send()
        return 0

    lax.fori_loop(0, items, drain_items, 0)

    def drain_groups(e, _):
        for m in range(14):
            ag(e, e, 1, m).wait_send()
            ag(experts + e, experts + 2 * e, 2, m).wait_send()
        for i in range(3):
            out_copy(i, e).wait()
        return 0

    lax.fori_loop(0, experts, drain_groups, 0)
    tk_drain(0)
    tk_drain(1)
    m_final(1, gt_out)
    m_drain(0)
    m_drain(1)


def body(tokens, routes, combine, w_gate, w_up, w_down, cotangent):
    experts, width, hidden = w_gate.shape
    half = hidden // 2
    total = routes.shape[0]
    block = tokens.shape[0]
    items = 3 * experts
    vm = pl.BlockSpec(memory_space=pltpu.VMEM)
    hbm = pl.BlockSpec(memory_space=pl.ANY)
    V = pltpu.VMEM
    DMA = pltpu.SemaphoreType.DMA
    scratch = [
        V((2, 2, experts, width, half), BF),
        V((2, experts, half, width), BF),
        V((2, 2, 8, width, block), BF),
        V((experts, CP, total), BF),
        V((experts, CP, 128), F32),
        V((2, experts, CP, width), BF),
        V((experts, width, CP), BF),
        V((items, 4, 2, ROWS, WA), BF),
        V((items, 4, 2, 2, ROWS, WB), BF),
        V((items, 4, 2, ROWS, WA), BF),
        V((items, 4, 2, 2, ROWS, WB), BF),
        V((items, 4, 2, ROWS, WA), BF),
        V((items, 4, 2, 2, ROWS, WB), BF),
        V((items, 2, ROWS, WA), BF),
        V((items, 2, 2, ROWS, WA), BF),
        V((items, ROWS, WA), BF),
        V((items, ROWS, WA), BF),
        V((items, 4, 2, ROWS, WB), BF),
        V((items, 2, ROWS, WB), BF),
        V((items, 2, 2, ROWS, WB), BF),
        V((2, experts, ROWS, WA), F32),
        V((2, experts, 2, ROWS, WB), F32),
        V((items, 2, 4, 2, ROWS, WA), BF),
        V((items, 2, 4, 2, 2, ROWS, WB), BF),
        V((2, experts, width, CP), BF),
        V((2, 2, 8, width, block), BF),
        V((2, 2, 4, 2, width, block), BF),
        V((2, width, block), BF),
        V((2, width, block), BF),
        V((experts, width, hidden), BF),
        V((experts, width, hidden), BF),
        V((experts, hidden, width), BF),
        V((CP, 256), F32),
        V((block, 256), F32),
        DMA((6,)),
        DMA((3, experts)),
        DMA((items, 12)),
        DMA((items, 12)),
        DMA((2 * experts, 14)),
        DMA((2 * experts, 14)),
        DMA((2, 17)),
        DMA((2, 17)),
        DMA((2, 9)),
        DMA((2, 9)),
    ]
    call = pl.pallas_call(
        kernel,
        out_shape=(
            jax.ShapeDtypeStruct(tokens.shape, BF),
            jax.ShapeDtypeStruct(tokens.shape, BF),
            jax.ShapeDtypeStruct(w_gate.shape, BF),
            jax.ShapeDtypeStruct(w_up.shape, BF),
            jax.ShapeDtypeStruct(w_down.shape, BF),
        ),
        in_specs=[vm, vm, vm, vm, hbm, hbm, hbm],
        out_specs=(vm, vm, hbm, hbm, hbm),
        scratch_shapes=scratch,
        compiler_params=pltpu.CompilerParams(
            collective_id=0, has_side_effects=True, vmem_limit_bytes=62 * 2**20
        ),
    )
    return call(tokens, cotangent, routes.T, combine.T, w_gate, w_up, w_down)


def solution(mesh):
    rows = P("expert", "dp")
    wide = P("expert", "dp", None)
    deep = P("expert", None, "dp")
    return jax.shard_map(
        body,
        mesh=mesh,
        in_specs=(rows, P(), P(), wide, wide, deep, rows),
        out_specs=(rows, rows, wide, wide, deep),
        check_vma=False,
    )
```

```python
import jax
import jax.numpy as jnp
from jax import lax
from jax.experimental import pallas as pl
from jax.experimental.pallas import tpu as pltpu
from jax.sharding import PartitionSpec as P

MESH = pl.DeviceIdType.MESH
BF = jnp.bfloat16
F32 = jnp.float32

SK = 1
CP = 384
ROWS = 48
WA = 384
WB = 128


def dot(a, b):
    return jnp.dot(a, b, preferred_element_type=F32)


def dot_nt(a, b):
    return lax.dot_general(a, b, (((1,), (1,)), ((), ())), preferred_element_type=F32)


def kernel(
    tok, cot, routes, combine, wg, wu, wd,
    mixed_out, gt_out, gg_out, gu_out, gd_out,
    W, TK, A, WT, WR, PK, PT, PSa, PSb, Qa, Qb, CRa, CRb,
    Y1a, Y2a, Xa, XSa, Xb, Y1b, Y2b, GUa, GUb, Fa, Fb,
    YT, MP, MR, MX, MXS, GS, TP,
    wsem, osem, rs_s, rs_r, ag_s, ag_r, tk_s, tk_r, m_s, m_r,
):
    experts, width = wg.shape[0], wg.shape[1]
    half = wg.shape[2] // 2
    tokens = routes.shape[1]
    d = lax.axis_index("dp")
    ex = lax.axis_index("expert")
    y, xh, c = d // 4, (d // 2) % 2, d % 2
    xl, z = ex // 8, ex % 8
    yr, yl, yo = (y + 1) % 4, (y + 3) % 4, (y + 2) % 4
    xo, co, xlo = 1 - xh, 1 - c, 1 - xl

    def dev(yy, xx, cc, ll, zz):
        return (yy * 4 + xx * 2 + cc, ll * 8 + zz)

    CORE = dev(y, xh, co, xl, z)
    YR = dev(yr, xh, c, xl, z)
    YL = dev(yl, xh, c, xl, z)
    XH = dev(y, xo, c, xl, z)
    XL = dev(y, xh, c, xlo, z)
    ZR = dev(y, xh, c, xl, (z + 1) % 8)
    ZL = dev(y, xh, c, xl, (z + 7) % 8)

    def remote(src, dst, ss, rr, to):
        return pltpu.make_async_remote_copy(
            src_ref=src, dst_ref=dst, send_sem=ss, recv_sem=rr,
            device_id=to, device_id_type=MESH,
        )

    def sent(ref, sem):
        remote(ref, ref, sem, sem, CORE).wait_send()

    def weight_copies():
        out = []
        for i, w in enumerate((wg, wu, wd)):
            for h in range(2):
                out.append(pltpu.make_async_copy(
                    w.at[:, :, pl.ds(h * half, half)], W.at[i, h], wsem.at[i * 2 + h]))
        return out

    barrier = pltpu.get_barrier_semaphore()
    for peer in (CORE, YR, YL, XH, XL, ZR, ZL):
        pl.semaphore_signal(barrier, inc=1, device_id=peer, device_id_type=MESH)
    for cp in weight_copies():
        cp.start()

    for i, src in enumerate((tok, cot)):
        TK[i, xl, z] = src[...]
    pl.semaphore_wait(barrier, 7)

    def tk_x(i):
        r = TK.at[i, xl, z]
        return remote(r, r, tk_s.at[i, 2], tk_r.at[i, 16], XL)

    def tk_z(i, way, s, b):
        zs = (z + 8 - (s - 1)) % 8 if way == 0 else (z + (s - 1)) % 8
        r = TK.at[i, b, zs]
        n = way * 8 + (s - 1) * 2 + b
        return remote(r, r, tk_s.at[i, way], tk_r.at[i, n], ZR if way == 0 else ZL)

    def tk0(i):
        tk_z(i, 0, 1, xl).start()
        tk_z(i, 1, 1, xl).start()
        tk_x(i).start()

    def tk1(i):
        tk_x(i).wait_recv()
        tk_z(i, 0, 1, xlo).start()
        tk_z(i, 1, 1, xlo).start()

    def tk_hop(i, s):
        if s < 3:
            for b in (xl, xlo):
                for way in (0, 1):
                    tk_z(i, way, s, b).wait_recv()
                    tk_z(i, way, s + 1, b).start()
        elif s == 3:
            for way in (0, 1):
                tk_z(i, way, 3, way).wait_recv()
                tk_z(i, way, 4, way).start()
            for way in (0, 1):
                tk_z(i, way, 3, 1 - way).wait_recv()
        else:
            for way in (0, 1):
                tk_z(i, way, 4, way).wait_recv()

    def tk_drain(i):
        tk_x(i).wait_send()
        for way in (0, 1):
            sent(TK.at[i, 0, pl.ds(0, 7)], tk_s.at[i, way])

    def token_rows(i):
        return jnp.concatenate([TK[i, n // 8, n % 8] for n in range(16)], axis=1)

    def m_z(i, way, s):
        zd = (z + 5 - s) % 8 if way == 0 else (z + 3 + s) % 8
        n = way * 4 + s - 1
        to = ZR if way == 0 else ZL
        if s == 1:
            return remote(MP.at[i, way, zd], MR.at[i, way, 0, way], m_s.at[i, way], m_r.at[i, n], to)
        return remote(MP.at[i, :, zd], MR.at[i, way, s - 1], m_s.at[i, way], m_r.at[i, n], to)

    def m_x(i):
        return remote(MXS.at[i], MX.at[i], m_s.at[i, 2], m_r.at[i, 8], XL)

    def m_partial(i):
        for q in range(4):
            acc = dot(YT[i, 0], A[0, :, q * 512:(q + 1) * 512])
            for e in range(1, experts):
                acc = acc + dot(YT[i, e], A[e, :, q * 512:(q + 1) * 512])
            acc = acc.astype(BF)
            for j in range(4):
                n = q * 4 + j
                MP[i, n // 8, n % 8] = acc[:, j * 128:(j + 1) * 128]
        m_z(i, 0, 1).start()
        m_z(i, 1, 1).start()

    def m_step(i, s):
        for way in (0, 1):
            zd = (z + 5 - s) % 8 if way == 0 else (z + 3 + s) % 8
            m_z(i, way, s - 1).wait_recv()
            if s == 2:
                MP[i, way, zd] = (MP[i, way, zd].astype(F32) + MR[i, way, 0, way].astype(F32)).astype(BF)
            else:
                for b in (0, 1):
                    MP[i, b, zd] = (MP[i, b, zd].astype(F32) + MR[i, way, s - 2, b].astype(F32)).astype(BF)
            m_z(i, way, s).start()

    def m_sum(i, b):
        return MP[i, b, z].astype(F32) + MR[i, 0, 3, b].astype(F32) + MR[i, 1, 3, b].astype(F32)

    def m_end(i):
        m_z(i, 0, 4).wait_recv()
        m_z(i, 1, 4).wait_recv()
        MXS[i] = m_sum(i, xlo).astype(BF)
        m_x(i).start()

    def m_final(i, out):
        m_x(i).wait_recv()
        out[...] = (m_sum(i, xl) + MX[i].astype(F32)).astype(BF)

    def m_drain(i):
        for way in (0, 1):
            sent(MP.at[i, 0, pl.ds(0, 7)], m_s.at[i, way])
        m_x(i).wait_send()

    def rs(k, n):
        s, r = rs_s.at[n], rs_r.at[k, n]
        if n == 0:
            return remote(PSa.at[k], CRa.at[k], s, r, CORE)
        if n == 1:
            return remote(PSb.at[k], CRb.at[k], s, r, CORE)
        if n == 2:
            return remote(Qa.at[k, yo, 0], Y1a.at[k, 0], s, r, YR)
        if n == 3:
            return remote(Qa.at[k, yo, 1], Y1a.at[k, 1], s, r, YL)
        if n == 4:
            return remote(Qa.at[k, yr], Y2a.at[k, 0], s, r, YR)
        if n == 5:
            return remote(Qa.at[k, yl], Y2a.at[k, 1], s, r, YL)
        if n == 6:
            return remote(XSa.at[k], Xa.at[k], s, r, XH)
        if n == 7:
            return remote(Qb.at[k, :, xo], Xb.at[k], s, r, XH)
        if n == 8:
            return remote(Qb.at[k, yo, xh, 0], Y1b.at[k, 0], s, r, YR)
        if n == 9:
            return remote(Qb.at[k, yo, xh, 1], Y1b.at[k, 1], s, r, YL)
        if n == 10:
            return remote(Qb.at[k, yr, xh], Y2b.at[k, 0], s, r, YR)
        return remote(Qb.at[k, yl, xh], Y2b.at[k, 1], s, r, YL)

    def put(ra, rb, k, v):
        v = v.astype(BF)
        ra[k] = v[:, :WA].reshape(4, 2, ROWS, WA)
        for p in range(2):
            rb[k, :, :, p] = v[:, WA + p * WB:WA + (p + 1) * WB].reshape(4, 2, ROWS, WB)

    def s0(k, part):
        put(PSa, PSb, k, part(co))
        rs(k, 0).start()
        rs(k, 1).start()
        put(Qa, Qb, k, part(c))

    def add(ref, idx, other):
        ref[idx] = (ref[idx].astype(F32) + other.astype(F32)).astype(BF)

    def s1(k):
        rs(k, 0).wait_recv()
        add(Qa, (k, yo), CRa[k, yo])
        rs(k, 2).start()
        rs(k, 3).start()
        rs(k, 1).wait_recv()
        for j in range(4):
            add(Qb, (k, j), CRb[k, j])
        rs(k, 7).start()
        for j in (yr, yl, y):
            add(Qa, (k, j), CRa[k, j])

    def s2(k):
        rs(k, 2).wait_recv()
        add(Qa, (k, yr, 0), Y1a[k, 0])
        rs(k, 4).start()
        rs(k, 3).wait_recv()
        add(Qa, (k, yl, 1), Y1a[k, 1])
        rs(k, 5).start()
        rs(k, 7).wait_recv()
        add(Qb, (k, yo, xh), Xb[k, yo])
        rs(k, 8).start()
        rs(k, 9).start()
        for j in (yr, yl, y):
            add(Qb, (k, j, xh), Xb[k, j])

    def sum_a(k, x):
        return Qa[k, y, x].astype(F32) + Y2a[k, 0, x].astype(F32) + Y2a[k, 1, x].astype(F32)

    def s3(k):
        rs(k, 8).wait_recv()
        add(Qb, (k, yr, xh, 0), Y1b[k, 0])
        rs(k, 10).start()
        rs(k, 9).wait_recv()
        add(Qb, (k, yl, xh, 1), Y1b[k, 1])
        rs(k, 11).start()
        rs(k, 4).wait_recv()
        rs(k, 5).wait_recv()
        XSa[k] = sum_a(k, xo).astype(BF)
        rs(k, 6).start()

    def s4(k):
        rs(k, 6).wait_recv()
        va = sum_a(k, xh) + Xa[k].astype(F32)
        rs(k, 10).wait_recv()
        rs(k, 11).wait_recv()
        vb = Qb[k, y, xh].astype(F32) + Y2b[k, 0].astype(F32) + Y2b[k, 1].astype(F32)
        return va, vb

    def hidden_of(gate, up):
        return (gate * jax.nn.sigmoid(gate) * up).astype(BF)

    def grads_of(back, gate, up):
        sg = jax.nn.sigmoid(gate)
        return (back * up * sg * (1.0 + gate * (1.0 - sg))).astype(BF), (back * gate * sg).astype(BF)

    def ag(g, j, n, m):
        s, r = ag_s.at[m], ag_r.at[g, m]
        js = pl.ds(j, n)
        if m == 0:
            ref, to = Fa.at[js, c, y, xh], XH
        elif m in (1, 2):
            ref, to = Fa.at[js, c, y, xh], (YR if m == 1 else YL)
        elif m in (3, 4):
            ref, to = Fa.at[js, c, y, xo], (YR if m == 3 else YL)
        elif m == 5:
            ref, to = Fa.at[js, c, yl, 0], YR
        elif m == 6:
            ref, to = Fa.at[js, c, yr, 1], YL
        elif m in (7, 8):
            ref, to = Fb.at[js, c, y, xh], (YR if m == 7 else YL)
        elif m == 9:
            ref, to = Fb.at[js, c, yl, xh, 0], YR
        elif m == 10:
            ref, to = Fb.at[js, c, yr, xh, 1], YL
        elif m == 11:
            ref, to = Fb.at[js, c, :, xh], XH
        elif m == 12:
            ref, to = Fa.at[js, c], CORE
        else:
            ref, to = Fb.at[js, c], CORE
        return remote(ref, ref, s, r, to)

    def ag_stage(i, g, j, n):
        if i == 0:
            for m in (0, 1, 2, 7, 8):
                ag(g, j, n, m).start()
        if i == 1:
            ag(g, j, n, 0).wait_recv()
            ag(g, j, n, 3).start()
            ag(g, j, n, 4).start()
            ag(g, j, n, 7).wait_recv()
            ag(g, j, n, 9).start()
            ag(g, j, n, 8).wait_recv()
            ag(g, j, n, 10).start()
        if i == 2:
            ag(g, j, n, 1).wait_recv()
            ag(g, j, n, 3).wait_recv()
            ag(g, j, n, 5).start()
            ag(g, j, n, 2).wait_recv()
            ag(g, j, n, 4).wait_recv()
            ag(g, j, n, 6).start()
            ag(g, j, n, 9).wait_recv()
            ag(g, j, n, 10).wait_recv()
            ag(g, j, n, 11).start()
        if i == 3:
            ag(g, j, n, 5).wait_recv()
            ag(g, j, n, 6).wait_recv()
            ag(g, j, n, 12).start()
            ag(g, j, n, 11).wait_recv()
            ag(g, j, n, 13).start()
        if i == 4:
            ag(g, j, n, 12).wait_recv()
            ag(g, j, n, 13).wait_recv()

    def full(j, h):
        return jnp.concatenate(
            [Fa[j, h].reshape(CP, WA), Fb[j, h, :, :, 0].reshape(CP, WB), Fb[j, h, :, :, 1].reshape(CP, WB)], axis=1)

    def out_copy(i, e):
        return pltpu.make_async_copy(GS.at[i, e], (gg_out, gu_out, gd_out)[i].at[e], osem.at[i])

    def turn(v):
        TP[:, :width] = v
        return jnp.transpose(TP[...])[:width].astype(BF)

    def use_hidden(e):
        acc = jnp.zeros((width, CP), F32)
        for h in range(2):
            f = full(e, h)
            acc = acc + dot_nt(W[2, h, e], f)
            GS[2, e, :, h * half:(h + 1) * half] = dot(PT[1, e], f).astype(BF)
        out_copy(2, e).start()
        YT[0, e] = (acc * WR[e, 0:1]).astype(BF)

    def use_grads(e):
        acc = jnp.zeros((width, CP), F32)
        for i in range(2):
            for h in range(2):
                f = full(experts + 2 * e + i, h)
                acc = acc + dot_nt(W[i, h, e], f)
                GS[i, e, :, h * half:(h + 1) * half] = dot(PT[0, e], f).astype(BF)
            out_copy(i, e).start()
        YT[1, e] = acc.astype(BF)

    tk0(0)
    TP[...] = jnp.zeros_like(TP)
    lane = lax.broadcasted_iota(jnp.int32, (1, tokens), 1)
    for e in range(experts):
        same = routes[...] == ex * experts + e
        routed = jnp.max(jnp.where(same, 1, 0), axis=0, keepdims=True)
        weight = jnp.sum(jnp.where(same, combine[...], 0.0), axis=0, keepdims=True)
        rank = jnp.broadcast_to(routed, (8, tokens))
        lanes = jnp.broadcast_to(lane, (8, tokens))
        step = 1
        while step < tokens:
            rank = rank + jnp.where(lanes >= step, pltpu.roll(rank, step, 1), 0)
            step *= 2
        pos = jnp.where(routed > 0, rank[0:1] - 1, -1)
        if e == 0:
            tk1(0)

        def fill(i, _, e=e, pos=pos, weight=weight):
            at = pl.ds(pl.multiple_of(i * 32, 32), 32)
            hit = lax.broadcasted_iota(jnp.int32, (32, tokens), 0) + i * 32 == pos
            A[e, at] = jnp.where(hit, 1.0, 0.0).astype(BF)
            WT[e, at] = jnp.broadcast_to(
                jnp.sum(jnp.where(hit, weight, 0.0), axis=1, keepdims=True), (32, 128))
            return 0

        lax.fori_loop(0, CP // 32, fill, 0)
        WR[e] = jnp.transpose(WT[e])
        tk_hop(0, e + 1)
    tk_hop(0, 4)
    for cp in weight_copies():
        cp.wait()
    rows = token_rows(0)
    for e in range(experts):
        v = dot_nt(A[e], rows)
        PK[0, e] = v.astype(BF)
        PT[0, e] = turn(v)

    gu = 2 * experts
    items = gu + experts
    ag_h = 1 + 4 * SK
    ag_p = gu + 4 * SK
    last = ag_p + experts - 1 + 4 * SK

    def tick(t, _):
        def at(k, lo, hi, f):
            @pl.when(jnp.logical_and(k >= lo, k < hi))
            def _():
                f(k)

        def on(k, f):
            @pl.when(t == k)
            def _():
                f()

        at(t, 0, gu, lambda k: s0(k, lambda h: dot(PK[0, k // 2], W[k % 2, h, k // 2])))
        at(t, gu, items, lambda k: s0(k, lambda h: dot(PK[1, k - gu], W[2, h, k - gu])))
        at(t - SK, 0, items, s1)
        at(t - 2 * SK, 0, items, s2)
        at(t - 3 * SK, 0, items, s3)

        def end(k):
            va, vb = s4(k)

            @pl.when(k < gu)
            def _():
                GUa[k % 2, k // 2] = va
                GUb[k % 2, k // 2] = vb

            @pl.when(jnp.logical_and(k < gu, k % 2 == 1))
            def _():
                e = k // 2
                Fa[e, c, y, xh] = hidden_of(GUa[0, e], va)
                Fb[e, c, y, xh] = hidden_of(GUb[0, e], vb)
                ag_stage(0, e, e, 1)

            @pl.when(k >= gu)
            def _():
                e = k - gu
                j = experts + 2 * e
                Fa[j, c, y, xh], Fa[j + 1, c, y, xh] = grads_of(va, GUa[0, e], GUa[1, e])
                Fb[j, c, y, xh], Fb[j + 1, c, y, xh] = grads_of(vb, GUb[0, e], GUb[1, e])
                ag_stage(0, experts + e, j, 2)

        at(t - 4 * SK, 0, items, end)

        for i in range(1, 5):
            u = t - ag_h - i * SK

            @pl.when(jnp.logical_and(jnp.logical_and(u >= 0, u < 2 * experts), u % 2 == 0))
            def _(u=u, i=i):
                e = u // 2
                ag_stage(i, e, e, 1)
                if i == 4:
                    use_hidden(e)

            def grads_stage(e, i=i):
                ag_stage(i, experts + e, experts + 2 * e, 2)
                if i == 4:
                    use_grads(e)

            at(t - ag_p - i * SK, 0, experts, grads_stage)

        on(0, lambda: tk0(1))
        on(1, lambda: tk1(1))
        on(2, lambda: tk_hop(1, 1))
        on(3, lambda: tk_hop(1, 2))
        on(4, lambda: tk_hop(1, 3))

        def cot_slots():
            tk_hop(1, 4)
            crow = token_rows(1)
            for e in range(experts):
                v = dot_nt(A[e], crow) * WT[e, :, 0:1]
                PK[1, e] = v.astype(BF)
                PT[1, e] = turn(v)

        on(gu - 1, cot_slots)
        m0 = ag_h + 2 * (experts - 1) + 4 * SK
        on(m0, lambda: m_partial(0))
        on(m0 + 1, lambda: m_step(0, 2))
        on(m0 + 2, lambda: m_step(0, 3))
        return 0

    lax.fori_loop(0, last + 1, tick, 0)

    m_partial(1)
    m_step(0, 4)
    m_step(1, 2)
    m_end(0)
    m_step(1, 3)
    m_final(0, mixed_out)
    m_step(1, 4)
    m_end(1)

    for n, ref in enumerate((
        PSa, PSb, Y1a.at[:, 0], Y1a.at[:, 1], Y2a.at[:, 0], Y2a.at[:, 1], XSa, Xb,
        Y1b.at[:, 0], Y1b.at[:, 1], Y2b.at[:, 0], Y2b.at[:, 1],
    )):
        sent(ref, rs_s.at[n])
    for m in range(14):
        if m < 7:
            ref = Fa.at[:, c, y, xh]
        elif m < 9:
            ref = Fb.at[:, c, y, xh]
        elif m < 11:
            ref = Fb.at[:, c, y, xh, 0]
        elif m == 11:
            ref = Fb.at[:, c, :, xh]
        else:
            ref = (Fa if m == 12 else Fb).at[:, c]
        sent(ref, ag_s.at[m])
    for i in range(3):
        pltpu.make_async_copy(GS.at[i], (gg_out, gu_out, gd_out)[i], osem.at[i]).wait()
    tk_drain(0)
    tk_drain(1)
    m_final(1, gt_out)
    m_drain(0)
    m_drain(1)


def copy_out(*refs):
    small, large, sem = refs[10:]
    into, out = [], []
    for i in range(5):
        src, dst = refs[i], refs[5 + i]
        if i < 2:
            into.append(pltpu.make_async_copy(src, small.at[i], sem.at[i, 0, 0]))
            out.append(pltpu.make_async_copy(small.at[i], dst, sem.at[i, 0, 1]))
        else:
            for e in range(src.shape[0]):
                into.append(pltpu.make_async_copy(src.at[e], large.at[i - 2, e], sem.at[i, e, 0]))
                out.append(pltpu.make_async_copy(large.at[i - 2, e], dst.at[e], sem.at[i, e, 1]))
    for cp in into:
        cp.start()
    for first, second in zip(into, out):
        first.wait()
        second.start()
    for cp in out:
        cp.wait()


def body(tokens, routes, combine, w_gate, w_up, w_down, cotangent):
    experts, width, hidden = w_gate.shape
    half = hidden // 2
    total = routes.shape[0]
    block = tokens.shape[0]
    items = 3 * experts
    vm = pl.BlockSpec(memory_space=pltpu.VMEM)
    hbm = pl.BlockSpec(memory_space=pl.ANY)
    V = pltpu.VMEM
    DMA = pltpu.SemaphoreType.DMA
    scratch = [
        V((3, 2, experts, width, half), BF),
        V((2, 2, 8, width, block), BF),
        V((experts, CP, total), BF),
        V((experts, CP, 128), F32),
        V((experts, 128, CP), F32),
        V((2, experts, CP, width), BF),
        V((2, experts, width, CP), BF),
        V((items, 4, 2, ROWS, WA), BF),
        V((items, 4, 2, 2, ROWS, WB), BF),
        V((items, 4, 2, ROWS, WA), BF),
        V((items, 4, 2, 2, ROWS, WB), BF),
        V((items, 4, 2, ROWS, WA), BF),
        V((items, 4, 2, 2, ROWS, WB), BF),
        V((items, 2, ROWS, WA), BF),
        V((items, 2, 2, ROWS, WA), BF),
        V((items, ROWS, WA), BF),
        V((items, ROWS, WA), BF),
        V((items, 4, 2, ROWS, WB), BF),
        V((items, 2, ROWS, WB), BF),
        V((items, 2, 2, ROWS, WB), BF),
        V((2, experts, ROWS, WA), F32),
        V((2, experts, 2, ROWS, WB), F32),
        V((items, 2, 4, 2, ROWS, WA), BF),
        V((items, 2, 4, 2, 2, ROWS, WB), BF),
        V((2, experts, width, CP), BF),
        V((2, 2, 8, width, block), BF),
        V((2, 2, 4, 2, width, block), BF),
        V((2, width, block), BF),
        V((2, width, block), BF),
        V((3, experts, width, hidden), BF),
        V((CP, 256), F32),
        DMA((6,)),
        DMA((3,)),
        DMA((12,)),
        DMA((items, 12)),
        DMA((14,)),
        DMA((2 * experts, 14)),
        DMA((2, 3)),
        DMA((2, 17)),
        DMA((2, 3)),
        DMA((2, 9)),
    ]
    small = jax.ShapeDtypeStruct((width, block), BF)
    large = jax.ShapeDtypeStruct(w_gate.shape, BF)
    call = pl.pallas_call(
        kernel,
        out_shape=(small, small, large, large, large),
        in_specs=[vm, vm, vm, vm, hbm, hbm, hbm],
        out_specs=(vm, vm, hbm, hbm, hbm),
        scratch_shapes=scratch,
        compiler_params=pltpu.CompilerParams(
            collective_id=0, has_side_effects=True, vmem_limit_bytes=62 * 2**20
        ),
    )
    results = call(
        tokens.T, cotangent.T, routes.T, combine.T, w_gate, w_up, jnp.swapaxes(w_down, 1, 2)
    )
    mixed, grad_tokens, grad_gate, grad_up, grad_down = pl.pallas_call(
        copy_out,
        out_shape=(small, small, large, large, large),
        in_specs=[hbm] * 5,
        out_specs=(hbm,) * 5,
        scratch_shapes=[
            V((2, width, block), BF),
            V((3, experts, width, hidden), BF),
            DMA((5, experts, 2)),
        ],
    )(*results)
    return mixed.T, grad_tokens.T, grad_gate, grad_up, jnp.swapaxes(grad_down, 1, 2)


def solution(mesh):
    rows = P("expert", "dp")
    wide = P("expert", "dp", None)
    deep = P("expert", None, "dp")
    return jax.shard_map(
        body,
        mesh=mesh,
        in_specs=(rows, P(), P(), wide, wide, deep, rows),
        out_specs=(rows, rows, wide, wide, deep),
        check_vma=False,
    )
```

```python
import jax
import jax.numpy as jnp
from jax import lax
from jax.experimental import pallas as pl
from jax.experimental.pallas import tpu as pltpu
from jax.sharding import PartitionSpec as P

MESH = pl.DeviceIdType.MESH
BF = jnp.bfloat16
F32 = jnp.float32

SUM_AT = (0, 1, 2, 3, 4)
GATHER_AT = (0, 1, 2, 3, 4)
CP = 384
ROWS = 48
WA = 384
WB = 128


def dot(a, b):
    return jnp.dot(a, b, preferred_element_type=F32)


def dot_nt(a, b):
    return lax.dot_general(a, b, (((1,), (1,)), ((), ())), preferred_element_type=F32)


def kernel(
    tok, cot, routes, combine, wg, wu, wd,
    mixed_out, gt_out, GS,
    W, TK, A, WT, WR, PK, PT, PSa, PSb, Qa, Qb, CRa, CRb,
    Y1a, Y2a, Xa, XSa, Xb, Y1b, Y2b, GUa, GUb, Fa, Fb,
    YT, MP, MR, MX, MXS, TP,
    wsem, rs_s, rs_r, ag_s, ag_r, tk_s, tk_r, m_s, m_r,
):
    experts, width = wg.shape[0], wg.shape[1]
    half = wg.shape[2] // 2
    tokens = routes.shape[1]
    d = lax.axis_index("dp")
    ex = lax.axis_index("expert")
    y, xh, c = d // 4, (d // 2) % 2, d % 2
    xl, z = ex // 8, ex % 8
    yr, yl, yo = (y + 1) % 4, (y + 3) % 4, (y + 2) % 4
    xo, co, xlo = 1 - xh, 1 - c, 1 - xl

    def dev(yy, xx, cc, ll, zz):
        return (yy * 4 + xx * 2 + cc, ll * 8 + zz)

    CORE = dev(y, xh, co, xl, z)
    YR = dev(yr, xh, c, xl, z)
    YL = dev(yl, xh, c, xl, z)
    XH = dev(y, xo, c, xl, z)
    XL = dev(y, xh, c, xlo, z)
    ZR = dev(y, xh, c, xl, (z + 1) % 8)
    ZL = dev(y, xh, c, xl, (z + 7) % 8)

    def remote(src, dst, ss, rr, to):
        return pltpu.make_async_remote_copy(
            src_ref=src, dst_ref=dst, send_sem=ss, recv_sem=rr,
            device_id=to, device_id_type=MESH,
        )

    def sent(ref, sem):
        remote(ref, ref, sem, sem, CORE).wait_send()

    def weight_copies():
        out = []
        for i, w in enumerate((wg, wu, wd)):
            for h in range(2):
                out.append(pltpu.make_async_copy(
                    w.at[:, :, pl.ds(h * half, half)], W.at[i, h], wsem.at[i * 2 + h]))
        return out

    barrier = pltpu.get_barrier_semaphore()
    for peer in (CORE, YR, YL, XH, XL, ZR, ZL):
        pl.semaphore_signal(barrier, inc=1, device_id=peer, device_id_type=MESH)
    for cp in weight_copies():
        cp.start()

    for i, src in enumerate((tok, cot)):
        for f in range(2):
            TK[i, xl, z, f] = src[f * (width // 2):(f + 1) * (width // 2)]
    pl.semaphore_wait(barrier, 7)

    def tk_x(i, f):
        r = TK.at[i, xl, z, f]
        return remote(r, r, tk_s.at[i, 2], tk_r.at[i, 32 + f], XL)

    def tk_z(i, way, s, b, f):
        zs = (z + 8 - (s - 1)) % 8 if way == 0 else (z + (s - 1)) % 8
        r = TK.at[i, b, zs, f]
        n = ((way * 4 + s - 1) * 2 + b) * 2 + f
        return remote(r, r, tk_s.at[i, way], tk_r.at[i, n], ZR if way == 0 else ZL)

    def tk0(i):
        for f in range(2):
            for way in (0, 1):
                tk_z(i, way, 1, xl, f).start()
            tk_x(i, f).start()

    def tk1(i):
        for f in range(2):
            tk_x(i, f).wait_recv()
            for way in (0, 1):
                tk_z(i, way, 1, xlo, f).start()

    def tk_hop(i, s):
        if s < 3:
            for b in (xl, xlo):
                for f in range(2):
                    for way in (0, 1):
                        tk_z(i, way, s, b, f).wait_recv()
                        tk_z(i, way, s + 1, b, f).start()
        elif s == 3:
            for f in range(2):
                for way in (0, 1):
                    tk_z(i, way, 3, way, f).wait_recv()
                    tk_z(i, way, 4, way, f).start()
            for f in range(2):
                for way in (0, 1):
                    tk_z(i, way, 3, 1 - way, f).wait_recv()
        else:
            for f in range(2):
                for way in (0, 1):
                    tk_z(i, way, 4, way, f).wait_recv()

    def tk_drain(i):
        sent(TK.at[i, 0, 0], tk_s.at[i, 2])
        for way in (0, 1):
            sent(TK.at[i, 0, pl.ds(0, 7)], tk_s.at[i, way])

    def token_rows(i):
        return jnp.concatenate([TK[i, n // 8, n % 8].reshape(width, 128) for n in range(16)], axis=1)

    def m_dest(way, s):
        return (z + 5 - s) % 8 if way == 0 else (z + 3 + s) % 8

    def m_z(i, way, s, b, f):
        n = ((way * 4 + s - 1) * 2 + b) * 2 + f
        return remote(
            MP.at[i, b, m_dest(way, s), f], MR.at[i, way, s - 1, b, f],
            m_s.at[i, way], m_r.at[i, n], ZR if way == 0 else ZL)

    def m_x(i, f):
        return remote(MXS.at[i, f], MX.at[i, f], m_s.at[i, 2], m_r.at[i, 32 + f], XL)

    def m_partial(i):
        for q in (2, 0, 3, 1):
            acc = dot(YT[i, 0], A[0, :, q * 512:(q + 1) * 512])
            for e in range(1, experts):
                acc = acc + dot(YT[i, e], A[e, :, q * 512:(q + 1) * 512])
            acc = acc.astype(BF)
            for j in range(4):
                n = q * 4 + j
                MP[i, n // 8, n % 8] = acc[:, j * 128:(j + 1) * 128].reshape(2, width // 2, 128)
        for f in range(2):
            for way in (0, 1):
                m_z(i, way, 1, way, f).start()
        for f in range(2):
            for way in (0, 1):
                m_z(i, way, 2, 1 - way, f).start()

    def m_add(i, way, s, b, f):
        m_z(i, way, s - 1, b, f).wait_recv()
        zd = m_dest(way, s)
        MP[i, b, zd, f] = (MP[i, b, zd, f].astype(F32) + MR[i, way, s - 2, b, f].astype(F32)).astype(BF)
        m_z(i, way, s, b, f).start()

    def m_step(i, s):
        for n in range(1 if s == 2 else 2):
            for f in range(2):
                for way in (0, 1):
                    m_add(i, way, s, way if n == 0 else 1 - way, f)

    def m_sum(i, b, f):
        m_z(i, 0, 4, b, f).wait_recv()
        m_z(i, 1, 4, b, f).wait_recv()
        return MP[i, b, z, f].astype(F32) + MR[i, 0, 3, b, f].astype(F32) + MR[i, 1, 3, b, f].astype(F32)

    def m_end(i):
        for f in range(2):
            MXS[i, f] = m_sum(i, xlo, f).astype(BF)
            m_x(i, f).start()

    def m_final(i, out):
        for f in range(2):
            own = m_sum(i, xl, f)
            m_x(i, f).wait_recv()
            out[f * (width // 2):(f + 1) * (width // 2)] = (own + MX[i, f].astype(F32)).astype(BF)

    def m_drain(i):
        for way in (0, 1):
            sent(MP.at[i, 0, pl.ds(0, 7)], m_s.at[i, way])
        sent(MXS.at[i], m_s.at[i, 2])

    def rs(k, n):
        s, r = rs_s.at[n], rs_r.at[k, n]
        if n == 0:
            return remote(PSa.at[k], CRa.at[k], s, r, CORE)
        if n == 1:
            return remote(PSb.at[k], CRb.at[k], s, r, CORE)
        if n == 2:
            return remote(Qa.at[k, yo, 0], Y1a.at[k, 0], s, r, YR)
        if n == 3:
            return remote(Qa.at[k, yo, 1], Y1a.at[k, 1], s, r, YL)
        if n == 4:
            return remote(Qa.at[k, yr], Y2a.at[k, 0], s, r, YR)
        if n == 5:
            return remote(Qa.at[k, yl], Y2a.at[k, 1], s, r, YL)
        if n == 6:
            return remote(XSa.at[k], Xa.at[k], s, r, XH)
        if n == 7:
            return remote(Qb.at[k, :, xo], Xb.at[k], s, r, XH)
        if n == 8:
            return remote(Qb.at[k, yo, xh, 0], Y1b.at[k, 0], s, r, YR)
        if n == 9:
            return remote(Qb.at[k, yo, xh, 1], Y1b.at[k, 1], s, r, YL)
        if n == 10:
            return remote(Qb.at[k, yr, xh], Y2b.at[k, 0], s, r, YR)
        return remote(Qb.at[k, yl, xh], Y2b.at[k, 1], s, r, YL)

    def put(ra, rb, k, v):
        v = v.astype(BF)
        ra[k] = v[:, :WA].reshape(4, 2, ROWS, WA)
        for p in range(2):
            rb[k, :, :, p] = v[:, WA + p * WB:WA + (p + 1) * WB].reshape(4, 2, ROWS, WB)

    def s0(k, part):
        put(PSa, PSb, k, part(co))
        rs(k, 0).start()
        rs(k, 1).start()
        put(Qa, Qb, k, part(c))

    def add(ref, idx, other):
        ref[idx] = (ref[idx].astype(F32) + other.astype(F32)).astype(BF)

    def s1(k):
        rs(k, 0).wait_recv()
        add(Qa, (k, yo), CRa[k, yo])
        rs(k, 2).start()
        rs(k, 3).start()
        rs(k, 1).wait_recv()
        for j in range(4):
            add(Qb, (k, j), CRb[k, j])
        rs(k, 7).start()
        for j in (yr, yl, y):
            add(Qa, (k, j), CRa[k, j])

    def s2(k):
        rs(k, 2).wait_recv()
        add(Qa, (k, yr, 0), Y1a[k, 0])
        rs(k, 4).start()
        rs(k, 3).wait_recv()
        add(Qa, (k, yl, 1), Y1a[k, 1])
        rs(k, 5).start()
        rs(k, 7).wait_recv()
        add(Qb, (k, yo, xh), Xb[k, yo])
        rs(k, 8).start()
        rs(k, 9).start()
        for j in (yr, yl, y):
            add(Qb, (k, j, xh), Xb[k, j])

    def sum_a(k, x):
        return Qa[k, y, x].astype(F32) + Y2a[k, 0, x].astype(F32) + Y2a[k, 1, x].astype(F32)

    def s3(k):
        rs(k, 8).wait_recv()
        add(Qb, (k, yr, xh, 0), Y1b[k, 0])
        rs(k, 10).start()
        rs(k, 9).wait_recv()
        add(Qb, (k, yl, xh, 1), Y1b[k, 1])
        rs(k, 11).start()
        rs(k, 4).wait_recv()
        rs(k, 5).wait_recv()
        XSa[k] = sum_a(k, xo).astype(BF)
        rs(k, 6).start()

    def s4(k):
        rs(k, 6).wait_recv()
        va = sum_a(k, xh) + Xa[k].astype(F32)
        rs(k, 10).wait_recv()
        rs(k, 11).wait_recv()
        vb = Qb[k, y, xh].astype(F32) + Y2b[k, 0].astype(F32) + Y2b[k, 1].astype(F32)
        return va, vb

    def hidden_of(gate, up):
        return (gate * jax.nn.sigmoid(gate) * up).astype(BF)

    def grads_of(back, gate, up):
        sg = jax.nn.sigmoid(gate)
        return (back * up * sg * (1.0 + gate * (1.0 - sg))).astype(BF), (back * gate * sg).astype(BF)

    def ag(g, j, n, m):
        s, r = ag_s.at[m], ag_r.at[g, m]
        js = pl.ds(j, n)
        if m == 0:
            ref, to = Fa.at[js, c, y, xh], XH
        elif m in (1, 2):
            ref, to = Fa.at[js, c, y, xh], (YR if m == 1 else YL)
        elif m in (3, 4):
            ref, to = Fa.at[js, c, y, xo], (YR if m == 3 else YL)
        elif m == 5:
            ref, to = Fa.at[js, c, yl, 0], YR
        elif m == 6:
            ref, to = Fa.at[js, c, yr, 1], YL
        elif m in (7, 8):
            ref, to = Fb.at[js, c, y, xh], (YR if m == 7 else YL)
        elif m == 9:
            ref, to = Fb.at[js, c, yl, xh, 0], YR
        elif m == 10:
            ref, to = Fb.at[js, c, yr, xh, 1], YL
        elif m == 11:
            ref, to = Fb.at[js, c, :, xh], XH
        elif m == 12:
            ref, to = Fa.at[js, c], CORE
        else:
            ref, to = Fb.at[js, c], CORE
        return remote(ref, ref, s, r, to)

    def ag_stage(i, g, j, n):
        if i == 0:
            for m in (0, 1, 2, 7, 8):
                ag(g, j, n, m).start()
        if i == 1:
            ag(g, j, n, 0).wait_recv()
            ag(g, j, n, 3).start()
            ag(g, j, n, 4).start()
            ag(g, j, n, 7).wait_recv()
            ag(g, j, n, 9).start()
            ag(g, j, n, 8).wait_recv()
            ag(g, j, n, 10).start()
        if i == 2:
            ag(g, j, n, 1).wait_recv()
            ag(g, j, n, 3).wait_recv()
            ag(g, j, n, 5).start()
            ag(g, j, n, 2).wait_recv()
            ag(g, j, n, 4).wait_recv()
            ag(g, j, n, 6).start()
            ag(g, j, n, 9).wait_recv()
            ag(g, j, n, 10).wait_recv()
            ag(g, j, n, 11).start()
        if i == 3:
            ag(g, j, n, 5).wait_recv()
            ag(g, j, n, 6).wait_recv()
            ag(g, j, n, 12).start()
            ag(g, j, n, 11).wait_recv()
            ag(g, j, n, 13).start()
        if i == 4:
            ag(g, j, n, 12).wait_recv()
            ag(g, j, n, 13).wait_recv()

    def full(j, h):
        return jnp.concatenate(
            [Fa[j, h].reshape(CP, WA), Fb[j, h, :, :, 0].reshape(CP, WB), Fb[j, h, :, :, 1].reshape(CP, WB)], axis=1)

    def turn(v):
        TP[:, :width] = v
        return jnp.transpose(TP[...])[:width].astype(BF)

    def use_hidden(e):
        acc = jnp.zeros((width, CP), F32)
        for h in range(2):
            f = full(e, h)
            acc = acc + dot_nt(W[2, h, e], f)
            GS[2, e, :, h * half:(h + 1) * half] = dot(PT[1, e], f).astype(BF)
        YT[0, e] = (acc * WR[e, 0:1]).astype(BF)

    def use_grads(e):
        acc = jnp.zeros((width, CP), F32)
        for i in range(2):
            for h in range(2):
                f = full(experts + 2 * e + i, h)
                acc = acc + dot_nt(W[i, h, e], f)
                GS[i, e, :, h * half:(h + 1) * half] = dot(PT[0, e], f).astype(BF)
        YT[1, e] = acc.astype(BF)

    tk0(0)
    TP[...] = jnp.zeros_like(TP)
    lane = lax.broadcasted_iota(jnp.int32, (1, tokens), 1)
    for e in range(experts):
        same = routes[...] == ex * experts + e
        routed = jnp.max(jnp.where(same, 1, 0), axis=0, keepdims=True)
        weight = jnp.sum(jnp.where(same, combine[...], 0.0), axis=0, keepdims=True)
        rank = jnp.broadcast_to(routed, (8, tokens))
        lanes = jnp.broadcast_to(lane, (8, tokens))
        step = 1
        while step < tokens:
            rank = rank + jnp.where(lanes >= step, pltpu.roll(rank, step, 1), 0)
            step *= 2
        pos = jnp.where(routed > 0, rank[0:1] - 1, -1)
        if e == 0:
            tk1(0)

        def fill(i, _, e=e, pos=pos, weight=weight):
            at = pl.ds(pl.multiple_of(i * 32, 32), 32)
            hit = lax.broadcasted_iota(jnp.int32, (32, tokens), 0) + i * 32 == pos
            A[e, at] = jnp.where(hit, 1.0, 0.0).astype(BF)
            WT[e, at] = jnp.broadcast_to(
                jnp.sum(jnp.where(hit, weight, 0.0), axis=1, keepdims=True), (32, 128))
            return 0

        lax.fori_loop(0, CP // 32, fill, 0)
        WR[e] = jnp.transpose(WT[e])
        tk_hop(0, e + 1)
    tk_hop(0, 4)
    for cp in weight_copies():
        cp.wait()
    rows = token_rows(0)
    for e in range(experts):
        v = dot_nt(A[e], rows)
        PK[0, e] = v.astype(BF)
        PT[0, e] = turn(v)

    gu = 2 * experts
    items = gu + experts
    ag_h = 1 + SUM_AT[4]
    ag_p = gu + SUM_AT[4]
    last = ag_p + experts - 1 + GATHER_AT[4]

    def tick(t, _):
        def at(k, lo, hi, f):
            @pl.when(jnp.logical_and(k >= lo, k < hi))
            def _():
                f(k)

        def on(k, f):
            @pl.when(t == k)
            def _():
                f()

        at(t, 0, gu, lambda k: s0(k, lambda h: dot(PK[0, k // 2], W[k % 2, h, k // 2])))
        at(t, gu, items, lambda k: s0(k, lambda h: dot(PK[1, k - gu], W[2, h, k - gu])))
        at(t - SUM_AT[1], 0, items, s1)
        at(t - SUM_AT[2], 0, items, s2)
        at(t - SUM_AT[3], 0, items, s3)

        def end(k):
            va, vb = s4(k)

            @pl.when(k < gu)
            def _():
                GUa[k % 2, k // 2] = va
                GUb[k % 2, k // 2] = vb

            @pl.when(jnp.logical_and(k < gu, k % 2 == 1))
            def _():
                e = k // 2
                Fa[e, c, y, xh] = hidden_of(GUa[0, e], va)
                Fb[e, c, y, xh] = hidden_of(GUb[0, e], vb)
                ag_stage(0, e, e, 1)

            @pl.when(k >= gu)
            def _():
                e = k - gu
                j = experts + 2 * e
                Fa[j, c, y, xh], Fa[j + 1, c, y, xh] = grads_of(va, GUa[0, e], GUa[1, e])
                Fb[j, c, y, xh], Fb[j + 1, c, y, xh] = grads_of(vb, GUb[0, e], GUb[1, e])
                ag_stage(0, experts + e, j, 2)

        at(t - SUM_AT[4], 0, items, end)

        for i in range(1, 5):
            u = t - ag_h - GATHER_AT[i]

            @pl.when(jnp.logical_and(jnp.logical_and(u >= 0, u < 2 * experts), u % 2 == 0))
            def _(u=u, i=i):
                e = u // 2
                ag_stage(i, e, e, 1)
                if i == 4:
                    use_hidden(e)

            def grads_stage(e, i=i):
                ag_stage(i, experts + e, experts + 2 * e, 2)
                if i == 4:
                    use_grads(e)

            at(t - ag_p - GATHER_AT[i], 0, experts, grads_stage)

        on(0, lambda: tk0(1))
        on(1, lambda: tk1(1))
        on(2, lambda: tk_hop(1, 1))
        on(3, lambda: tk_hop(1, 2))
        on(4, lambda: tk_hop(1, 3))

        def cot_slots():
            tk_hop(1, 4)
            crow = token_rows(1)
            for e in range(experts):
                v = dot_nt(A[e], crow) * WT[e, :, 0:1]
                PK[1, e] = v.astype(BF)
                PT[1, e] = turn(v)

        on(gu - 1, cot_slots)
        m0 = ag_h + 2 * (experts - 1) + GATHER_AT[4]
        on(m0, lambda: m_partial(0))
        on(m0 + 1, lambda: m_step(0, 2))
        on(m0 + 2, lambda: m_step(0, 3))
        return 0

    lax.fori_loop(0, last + 1, tick, 0)

    m_partial(1)
    m_step(0, 4)
    m_step(1, 2)
    m_end(0)
    m_step(1, 3)
    m_final(0, mixed_out)
    m_step(1, 4)
    m_end(1)

    for n, ref in enumerate((
        PSa, PSb, Y1a.at[:, 0], Y1a.at[:, 1], Y2a.at[:, 0], Y2a.at[:, 1], XSa, Xb,
        Y1b.at[:, 0], Y1b.at[:, 1], Y2b.at[:, 0], Y2b.at[:, 1],
    )):
        sent(ref, rs_s.at[n])
    for m in range(14):
        if m < 7:
            ref = Fa.at[:, c, y, xh]
        elif m < 9:
            ref = Fb.at[:, c, y, xh]
        elif m < 11:
            ref = Fb.at[:, c, y, xh, 0]
        elif m == 11:
            ref = Fb.at[:, c, :, xh]
        else:
            ref = (Fa if m == 12 else Fb).at[:, c]
        sent(ref, ag_s.at[m])
    tk_drain(0)
    tk_drain(1)
    m_final(1, gt_out)
    m_drain(0)
    m_drain(1)


def copy_out(mixed, grad_tokens, grads, mixed_out, gt_out, gg_out, gu_out, gd_out, sem):
    copies = [
        pltpu.make_async_copy(mixed, mixed_out, sem.at[0]),
        pltpu.make_async_copy(grad_tokens, gt_out, sem.at[1]),
    ]
    for i, out in enumerate((gg_out, gu_out, gd_out)):
        for e in range(out.shape[0]):
            for h in range(2):
                rows = pl.ds(h * (out.shape[1] // 2), out.shape[1] // 2)
                copies.append(pltpu.make_async_copy(grads.at[i, e, rows], out.at[e, rows], sem.at[len(copies)]))
    for cp in copies:
        cp.start()
    for cp in copies:
        cp.wait()


def body(tokens, routes, combine, w_gate, w_up, w_down, cotangent):
    experts, width, hidden = w_gate.shape
    half = hidden // 2
    total = routes.shape[0]
    block = tokens.shape[0]
    items = 3 * experts
    vm = pl.BlockSpec(memory_space=pltpu.VMEM)
    hbm = pl.BlockSpec(memory_space=pl.ANY)
    V = pltpu.VMEM
    DMA = pltpu.SemaphoreType.DMA
    scratch = [
        V((3, 2, experts, width, half), BF),
        V((2, 2, 8, 2, width // 2, block), BF),
        V((experts, CP, total), BF),
        V((experts, CP, 128), F32),
        V((experts, 128, CP), F32),
        V((2, experts, CP, width), BF),
        V((2, experts, width, CP), BF),
        V((items, 4, 2, ROWS, WA), BF),
        V((items, 4, 2, 2, ROWS, WB), BF),
        V((items, 4, 2, ROWS, WA), BF),
        V((items, 4, 2, 2, ROWS, WB), BF),
        V((items, 4, 2, ROWS, WA), BF),
        V((items, 4, 2, 2, ROWS, WB), BF),
        V((items, 2, ROWS, WA), BF),
        V((items, 2, 2, ROWS, WA), BF),
        V((items, ROWS, WA), BF),
        V((items, ROWS, WA), BF),
        V((items, 4, 2, ROWS, WB), BF),
        V((items, 2, ROWS, WB), BF),
        V((items, 2, 2, ROWS, WB), BF),
        V((2, experts, ROWS, WA), F32),
        V((2, experts, 2, ROWS, WB), F32),
        V((items, 2, 4, 2, ROWS, WA), BF),
        V((items, 2, 4, 2, 2, ROWS, WB), BF),
        V((2, experts, width, CP), BF),
        V((2, 2, 8, 2, width // 2, block), BF),
        V((2, 2, 4, 2, 2, width // 2, block), BF),
        V((2, 2, width // 2, block), BF),
        V((2, 2, width // 2, block), BF),
        V((CP, 256), F32),
        DMA((6,)),
        DMA((12,)),
        DMA((items, 12)),
        DMA((14,)),
        DMA((2 * experts, 14)),
        DMA((2, 3)),
        DMA((2, 34)),
        DMA((2, 3)),
        DMA((2, 34)),
    ]
    small = jax.ShapeDtypeStruct((width, block), BF)
    large = jax.ShapeDtypeStruct(w_gate.shape, BF)
    call = pl.pallas_call(
        kernel,
        out_shape=(V((width, block), BF), V((width, block), BF), V((3, experts, width, hidden), BF)),
        in_specs=[vm, vm, vm, vm, hbm, hbm, hbm],
        out_specs=(vm, vm, vm),
        scratch_shapes=scratch,
        compiler_params=pltpu.CompilerParams(
            collective_id=0, has_side_effects=True, vmem_limit_bytes=55 * 2**20
        ),
    )
    results = call(
        tokens.T, cotangent.T, routes.T, combine.T, w_gate, w_up, jnp.swapaxes(w_down, 1, 2)
    )
    mixed, grad_tokens, grad_gate, grad_up, grad_down = pl.pallas_call(
        copy_out,
        out_shape=(small, small, large, large, large),
        in_specs=[vm] * 3,
        out_specs=(hbm,) * 5,
        scratch_shapes=[DMA((2 + 6 * experts,))],
        compiler_params=pltpu.CompilerParams(vmem_limit_bytes=2**20),
    )(*(pltpu.with_memory_space_constraint(r, pltpu.VMEM) for r in results))
    return mixed.T, grad_tokens.T, grad_gate, grad_up, jnp.swapaxes(grad_down, 1, 2)


def solution(mesh):
    rows = P("expert", "dp")
    wide = P("expert", "dp", None)
    deep = P("expert", None, "dp")
    return jax.shard_map(
        body,
        mesh=mesh,
        in_specs=(rows, P(), P(), wide, wide, deep, rows),
        out_specs=(rows, rows, wide, wide, deep),
        check_vma=False,
    )
```

```python
import jax
import jax.numpy as jnp
from jax import lax
from jax.experimental import pallas as pl
from jax.experimental.pallas import tpu as pltpu
from jax.sharding import PartitionSpec as P

MESH = pl.DeviceIdType.MESH
BF = jnp.bfloat16
F32 = jnp.float32

SUM_AT = (0, 1, 2, 3, 4)
GATHER_AT = (0, 1, 2, 3, 4)
CP = 384
ROWS = 48
WA = 384
WB = 128


def dot(a, b):
    return jnp.dot(a, b, preferred_element_type=F32)


def dot_nt(a, b):
    return lax.dot_general(a, b, (((1,), (1,)), ((), ())), preferred_element_type=F32)


def kernel(
    tok, cot, routes, combine, wg, wu, wd,
    mixed_out, gt_out, GS,
    W, TK, A, WT, WR, PK, PT, PSa, PSb, Qa, Qb, CRa, CRb,
    Y1a, Y2a, Xa, XSa, Xb, Y1b, Y2b, GUa, GUb, Fa, Fb,
    YT, MP, MR, MX, MXS, TP,
    wsem, rs_s, rs_r, ag_s, ag_r, tk_s, tk_r, m_s, m_r,
):
    experts, width = wg.shape[0], wg.shape[1]
    half = wg.shape[2] // 2
    tokens = routes.shape[1]
    d = lax.axis_index("dp")
    ex = lax.axis_index("expert")
    y, xh, c = d // 4, (d // 2) % 2, d % 2
    xl, z = ex // 8, ex % 8
    yr, yl, yo = (y + 1) % 4, (y + 3) % 4, (y + 2) % 4
    xo, co, xlo = 1 - xh, 1 - c, 1 - xl

    def dev(yy, xx, cc, ll, zz):
        return (yy * 4 + xx * 2 + cc, ll * 8 + zz)

    CORE = dev(y, xh, co, xl, z)
    YR = dev(yr, xh, c, xl, z)
    YL = dev(yl, xh, c, xl, z)
    XH = dev(y, xo, c, xl, z)
    XL = dev(y, xh, c, xlo, z)
    ZR = dev(y, xh, c, xl, (z + 1) % 8)
    ZL = dev(y, xh, c, xl, (z + 7) % 8)

    def remote(src, dst, ss, rr, to):
        return pltpu.make_async_remote_copy(
            src_ref=src, dst_ref=dst, send_sem=ss, recv_sem=rr,
            device_id=to, device_id_type=MESH,
        )

    def came(ref, sem):
        remote(ref, ref, sem, sem, CORE).wait_recv()

    def sent(ref, sem):
        remote(ref, ref, sem, sem, CORE).wait_send()

    def weight_copies():
        out = []
        for i, w in enumerate((wg, wu, wd)):
            for h in range(2):
                out.append(pltpu.make_async_copy(
                    w.at[:, :, pl.ds(h * half, half)], W.at[i, h], wsem.at[i * 2 + h]))
        return out

    barrier = pltpu.get_barrier_semaphore()
    for peer in (CORE, YR, YL, XH, XL, ZR, ZL):
        pl.semaphore_signal(barrier, inc=1, device_id=peer, device_id_type=MESH)
    for cp in weight_copies():
        cp.start()

    for i, src in enumerate((tok, cot)):
        for f in range(2):
            TK[i, xl, z, f] = src[f * (width // 2):(f + 1) * (width // 2)]
    pl.semaphore_wait(barrier, 7)

    def tk_x(i, f):
        r = TK.at[i, xl, z, f]
        return remote(r, r, tk_s.at[i, 2], tk_r.at[i, 32 + f], XL)

    def tk_z(i, way, s, b, f):
        zs = (z + 8 - (s - 1)) % 8 if way == 0 else (z + (s - 1)) % 8
        r = TK.at[i, b, zs, f]
        n = ((way * 4 + s - 1) * 2 + b) * 2 + f
        return remote(r, r, tk_s.at[i, way], tk_r.at[i, n], ZR if way == 0 else ZL)

    def tk0(i):
        for f in range(2):
            for way in (0, 1):
                tk_z(i, way, 1, xl, f).start()
            tk_x(i, f).start()

    def tk1(i):
        for f in range(2):
            tk_x(i, f).wait_recv()
            for way in (0, 1):
                tk_z(i, way, 1, xlo, f).start()

    def tk_hop(i, s):
        if s < 3:
            for b in (xl, xlo):
                for f in range(2):
                    for way in (0, 1):
                        tk_z(i, way, s, b, f).wait_recv()
                        tk_z(i, way, s + 1, b, f).start()
        elif s == 3:
            for f in range(2):
                for way in (0, 1):
                    tk_z(i, way, 3, way, f).wait_recv()
                    tk_z(i, way, 4, way, f).start()
            for f in range(2):
                for way in (0, 1):
                    tk_z(i, way, 3, 1 - way, f).wait_recv()
        else:
            for f in range(2):
                for way in (0, 1):
                    tk_z(i, way, 4, way, f).wait_recv()

    def tk_drain(i):
        sent(TK.at[i, 0, 0], tk_s.at[i, 2])
        for way in (0, 1):
            sent(TK.at[i, 0, pl.ds(0, 7)], tk_s.at[i, way])

    def token_rows(i):
        return jnp.concatenate([TK[i, n // 8, n % 8].reshape(width, 128) for n in range(16)], axis=1)

    def m_dest(way, s):
        return (z + 5 - s) % 8 if way == 0 else (z + 3 + s) % 8

    def m_z(i, way, s, b, f):
        n = ((way * 4 + s - 1) * 2 + b) * 2 + f
        return remote(
            MP.at[i, b, m_dest(way, s), f], MR.at[i, way, s - 1, b, f],
            m_s.at[i, way], m_r.at[i, n], ZR if way == 0 else ZL)

    def m_x(i, f):
        return remote(MXS.at[i, f], MX.at[i, f], m_s.at[i, 2], m_r.at[i, 32 + f], XL)

    def m_partial(i):
        for q in (2, 0, 3, 1):
            acc = dot(YT[i, 0], A[0, :, q * 512:(q + 1) * 512])
            for e in range(1, experts):
                acc = acc + dot(YT[i, e], A[e, :, q * 512:(q + 1) * 512])
            acc = acc.astype(BF)
            for j in range(4):
                n = q * 4 + j
                MP[i, n // 8, n % 8] = acc[:, j * 128:(j + 1) * 128].reshape(2, width // 2, 128)
        for f in range(2):
            for way in (0, 1):
                m_z(i, way, 1, way, f).start()
        for f in range(2):
            for way in (0, 1):
                m_z(i, way, 2, 1 - way, f).start()

    def m_add(i, way, s, b, f):
        m_z(i, way, s - 1, b, f).wait_recv()
        zd = m_dest(way, s)
        MP[i, b, zd, f] = (MP[i, b, zd, f].astype(F32) + MR[i, way, s - 2, b, f].astype(F32)).astype(BF)
        m_z(i, way, s, b, f).start()

    def m_step(i, s):
        for n in range(1 if s == 2 else 2):
            for f in range(2):
                for way in (0, 1):
                    m_add(i, way, s, way if n == 0 else 1 - way, f)

    def m_sum(i, b, f):
        m_z(i, 0, 4, b, f).wait_recv()
        m_z(i, 1, 4, b, f).wait_recv()
        return MP[i, b, z, f].astype(F32) + MR[i, 0, 3, b, f].astype(F32) + MR[i, 1, 3, b, f].astype(F32)

    def m_end(i):
        for f in range(2):
            MXS[i, f] = m_sum(i, xlo, f).astype(BF)
            m_x(i, f).start()

    def m_final(i, out):
        for f in range(2):
            own = m_sum(i, xl, f)
            m_x(i, f).wait_recv()
            out[f * (width // 2):(f + 1) * (width // 2)] = (own + MX[i, f].astype(F32)).astype(BF)

    def m_drain(i):
        for way in (0, 1):
            sent(MP.at[i, 0, pl.ds(0, 7)], m_s.at[i, way])
        sent(MXS.at[i], m_s.at[i, 2])

    def rs(k, n):
        s, r = rs_s.at[n], rs_r.at[k, {5: 4, 11: 10}.get(n, n)]
        if n == 0:
            return remote(PSa.at[k], CRa.at[k], s, r, CORE)
        if n == 1:
            return remote(PSb.at[k], CRb.at[k], s, r, CORE)
        if n == 2:
            return remote(Qa.at[k, yo, 0], Y1a.at[k, 0], s, r, YR)
        if n == 3:
            return remote(Qa.at[k, yo, 1], Y1a.at[k, 1], s, r, YL)
        if n == 4:
            return remote(Qa.at[k, yr], Y2a.at[k, 0], s, r, YR)
        if n == 5:
            return remote(Qa.at[k, yl], Y2a.at[k, 1], s, r, YL)
        if n == 6:
            return remote(XSa.at[k], Xa.at[k], s, r, XH)
        if n == 7:
            return remote(Qb.at[k, :, xo], Xb.at[k], s, r, XH)
        if n == 8:
            return remote(Qb.at[k, yo, xh, 0], Y1b.at[k, 0], s, r, YR)
        if n == 9:
            return remote(Qb.at[k, yo, xh, 1], Y1b.at[k, 1], s, r, YL)
        if n == 10:
            return remote(Qb.at[k, yr, xh], Y2b.at[k, 0], s, r, YR)
        return remote(Qb.at[k, yl, xh], Y2b.at[k, 1], s, r, YL)

    def put(ra, rb, k, v):
        v = v.astype(BF)
        ra[k] = v[:, :WA].reshape(4, 2, ROWS, WA)
        for p in range(2):
            rb[k, :, :, p] = v[:, WA + p * WB:WA + (p + 1) * WB].reshape(4, 2, ROWS, WB)

    def s0(k, part):
        put(PSa, PSb, k, part(co))
        rs(k, 0).start()
        rs(k, 1).start()
        put(Qa, Qb, k, part(c))

    def add(ref, idx, other):
        ref[idx] = (ref[idx].astype(F32) + other.astype(F32)).astype(BF)

    def s1(k):
        rs(k, 0).wait_recv()
        add(Qa, (k, yo), CRa[k, yo])
        rs(k, 2).start()
        rs(k, 3).start()
        rs(k, 1).wait_recv()
        for j in range(4):
            add(Qb, (k, j), CRb[k, j])
        rs(k, 7).start()
        for j in (yr, yl, y):
            add(Qa, (k, j), CRa[k, j])

    def s2(k):
        rs(k, 2).wait_recv()
        add(Qa, (k, yr, 0), Y1a[k, 0])
        rs(k, 4).start()
        rs(k, 3).wait_recv()
        add(Qa, (k, yl, 1), Y1a[k, 1])
        rs(k, 5).start()
        rs(k, 7).wait_recv()
        add(Qb, (k, yo, xh), Xb[k, yo])
        rs(k, 8).start()
        rs(k, 9).start()
        for j in (yr, yl, y):
            add(Qb, (k, j, xh), Xb[k, j])

    def sum_a(k, x):
        return Qa[k, y, x].astype(F32) + Y2a[k, 0, x].astype(F32) + Y2a[k, 1, x].astype(F32)

    def s3(k):
        rs(k, 8).wait_recv()
        add(Qb, (k, yr, xh, 0), Y1b[k, 0])
        rs(k, 10).start()
        rs(k, 9).wait_recv()
        add(Qb, (k, yl, xh, 1), Y1b[k, 1])
        rs(k, 11).start()
        came(Y2a.at[k], rs_r.at[k, 4])
        XSa[k] = sum_a(k, xo).astype(BF)
        rs(k, 6).start()

    def s4(k):
        rs(k, 6).wait_recv()
        va = sum_a(k, xh) + Xa[k].astype(F32)
        came(Y2b.at[k], rs_r.at[k, 10])
        vb = Qb[k, y, xh].astype(F32) + Y2b[k, 0].astype(F32) + Y2b[k, 1].astype(F32)
        return va, vb

    def hidden_of(gate, up):
        return (gate * jax.nn.sigmoid(gate) * up).astype(BF)

    def grads_of(back, gate, up):
        sg = jax.nn.sigmoid(gate)
        return (back * up * sg * (1.0 + gate * (1.0 - sg))).astype(BF), (back * gate * sg).astype(BF)

    def ag(g, j, n, m):
        s, r = ag_s.at[m], ag_r.at[g, (0, 1, 1, 1, 1, 2, 2, 3, 3, 4, 4, 5, 6, 7)[m]]
        js = pl.ds(j, n)
        if m == 0:
            ref, to = Fa.at[js, c, y, xh], XH
        elif m in (1, 2):
            ref, to = Fa.at[js, c, y, xh], (YR if m == 1 else YL)
        elif m in (3, 4):
            ref, to = Fa.at[js, c, y, xo], (YR if m == 3 else YL)
        elif m == 5:
            ref, to = Fa.at[js, c, yl, 0], YR
        elif m == 6:
            ref, to = Fa.at[js, c, yr, 1], YL
        elif m in (7, 8):
            ref, to = Fb.at[js, c, y, xh], (YR if m == 7 else YL)
        elif m == 9:
            ref, to = Fb.at[js, c, yl, xh, 0], YR
        elif m == 10:
            ref, to = Fb.at[js, c, yr, xh, 1], YL
        elif m == 11:
            ref, to = Fb.at[js, c, :, xh], XH
        elif m == 12:
            ref, to = Fa.at[js, c], CORE
        else:
            ref, to = Fb.at[js, c], CORE
        return remote(ref, ref, s, r, to)

    def ag_stage(i, g, j, n):
        js = pl.ds(j, n)
        if i == 0:
            for m in (0, 1, 2, 7, 8):
                ag(g, j, n, m).start()
        if i == 1:
            ag(g, j, n, 0).wait_recv()
            ag(g, j, n, 3).start()
            ag(g, j, n, 4).start()
            came(Fb.at[js, c, 0], ag_r.at[g, 3])
            ag(g, j, n, 9).start()
            ag(g, j, n, 10).start()
        if i == 2:
            came(Fa.at[js, c, pl.ds(0, 2)], ag_r.at[g, 1])
            ag(g, j, n, 5).start()
            ag(g, j, n, 6).start()
            came(Fb.at[js, c, 0, 0], ag_r.at[g, 4])
            ag(g, j, n, 11).start()
        if i == 3:
            came(Fa.at[js, c, 0], ag_r.at[g, 2])
            ag(g, j, n, 12).start()
            ag(g, j, n, 11).wait_recv()
            ag(g, j, n, 13).start()
        if i == 4:
            ag(g, j, n, 12).wait_recv()
            ag(g, j, n, 13).wait_recv()

    def full(j, h):
        return jnp.concatenate(
            [Fa[j, h].reshape(CP, WA), Fb[j, h, :, :, 0].reshape(CP, WB), Fb[j, h, :, :, 1].reshape(CP, WB)], axis=1)

    def turn(v):
        TP[:, :width] = v
        return jnp.transpose(TP[...])[:width].astype(BF)

    def use_hidden(e):
        acc = jnp.zeros((width, CP), F32)
        for h in range(2):
            f = full(e, h)
            acc = acc + dot_nt(W[2, h, e], f)
            GS[2, e, :, h * half:(h + 1) * half] = dot(PT[1, e], f).astype(BF)
        YT[0, e] = (acc * WR[e, 0:1]).astype(BF)

    def use_grads(e):
        acc = jnp.zeros((width, CP), F32)
        for i in range(2):
            for h in range(2):
                acc = acc + dot_nt(W[i, h, e], full(experts + 2 * e + i, h))
        YT[1, e] = acc.astype(BF)

    def weight_grads(e):
        for i in range(2):
            for h in range(2):
                f = full(experts + 2 * e + i, h)
                GS[i, e, :, h * half:(h + 1) * half] = dot(PT[0, e], f).astype(BF)

    tk0(0)
    TP[...] = jnp.zeros_like(TP)
    lane = lax.broadcasted_iota(jnp.int32, (1, tokens), 1)
    for e in range(experts):
        same = routes[...] == ex * experts + e
        routed = jnp.max(jnp.where(same, 1, 0), axis=0, keepdims=True)
        weight = jnp.sum(jnp.where(same, combine[...], 0.0), axis=0, keepdims=True)
        rank = jnp.broadcast_to(routed, (8, tokens))
        lanes = jnp.broadcast_to(lane, (8, tokens))
        step = 1
        while step < tokens:
            rank = rank + jnp.where(lanes >= step, pltpu.roll(rank, step, 1), 0)
            step *= 2
        pos = jnp.where(routed > 0, rank[0:1] - 1, -1)
        if e == 0:
            tk1(0)

        def fill(i, _, e=e, pos=pos, weight=weight):
            at = pl.ds(pl.multiple_of(i * 32, 32), 32)
            hit = lax.broadcasted_iota(jnp.int32, (32, tokens), 0) + i * 32 == pos
            A[e, at] = jnp.where(hit, 1.0, 0.0).astype(BF)
            WT[e, at] = jnp.broadcast_to(
                jnp.sum(jnp.where(hit, weight, 0.0), axis=1, keepdims=True), (32, 128))
            return 0

        lax.fori_loop(0, CP // 32, fill, 0)
        WR[e] = jnp.transpose(WT[e])
        tk_hop(0, e + 1)
    tk_hop(0, 4)
    for cp in weight_copies():
        cp.wait()

    def pick(e):
        v = dot_nt(A[e], token_rows(0))
        PK[0, e] = v.astype(BF)
        PT[0, e] = turn(v)

    pick(0)

    gu = 2 * experts
    items = gu + experts
    ag_h = 1 + SUM_AT[4]
    ag_p = gu + SUM_AT[4]
    last = ag_p + experts - 1 + GATHER_AT[4]

    def tick(t, _):
        def at(k, lo, hi, f):
            @pl.when(jnp.logical_and(k >= lo, k < hi))
            def _():
                f(k)

        def on(k, f):
            @pl.when(t == k)
            def _():
                f()

        at(t, 0, gu, lambda k: s0(k, lambda h: dot(PK[0, k // 2], W[k % 2, h, k // 2])))
        at(t, gu, items, lambda k: s0(k, lambda h: dot(PK[1, k - gu], W[2, h, k - gu])))
        at(t - SUM_AT[1], 0, items, s1)
        at(t - SUM_AT[2], 0, items, s2)
        at(t - SUM_AT[3], 0, items, s3)

        def end(k):
            va, vb = s4(k)

            @pl.when(k < gu)
            def _():
                GUa[k % 2, k // 2] = va
                GUb[k % 2, k // 2] = vb

            @pl.when(jnp.logical_and(k < gu, k % 2 == 1))
            def _():
                e = k // 2
                Fa[e, c, y, xh] = hidden_of(GUa[0, e], va)
                Fb[e, c, y, xh] = hidden_of(GUb[0, e], vb)
                ag_stage(0, e, e, 1)

            @pl.when(k >= gu)
            def _():
                e = k - gu
                j = experts + 2 * e
                Fa[j, c, y, xh], Fa[j + 1, c, y, xh] = grads_of(va, GUa[0, e], GUa[1, e])
                Fb[j, c, y, xh], Fb[j + 1, c, y, xh] = grads_of(vb, GUb[0, e], GUb[1, e])
                ag_stage(0, j, j, 1)
                ag_stage(0, j + 1, j + 1, 1)

        at(t - SUM_AT[4], 0, items, end)

        for i in range(1, 5):
            u = t - ag_h - GATHER_AT[i]

            @pl.when(jnp.logical_and(jnp.logical_and(u >= 0, u < 2 * experts), u % 2 == 0))
            def _(u=u, i=i):
                e = u // 2
                ag_stage(i, e, e, 1)
                if i == 4:
                    use_hidden(e)

            def grads_stage(e, i=i):
                ag_stage(i, experts + 2 * e, experts + 2 * e, 1)
                ag_stage(i, experts + 2 * e + 1, experts + 2 * e + 1, 1)
                if i == 4:
                    use_grads(e)

                    @pl.when(e < experts - 1)
                    def _():
                        weight_grads(e)

            at(t - ag_p - GATHER_AT[i], 0, experts, grads_stage)

        for e in range(1, experts):
            on(e - 1, lambda e=e: pick(e))
        on(0, lambda: tk0(1))
        on(1, lambda: tk1(1))
        on(2, lambda: tk_hop(1, 1))
        on(3, lambda: tk_hop(1, 2))
        on(4, lambda: tk_hop(1, 3))

        def cot_slots():
            tk_hop(1, 4)
            crow = token_rows(1)
            for e in range(experts):
                v = dot_nt(A[e], crow) * WT[e, :, 0:1]
                PK[1, e] = v.astype(BF)
                PT[1, e] = turn(v)

        on(gu - 1, cot_slots)
        m0 = ag_h + 2 * (experts - 1) + GATHER_AT[4]
        on(m0, lambda: m_partial(0))
        on(m0 + 1, lambda: m_step(0, 2))
        on(m0 + 2, lambda: m_step(0, 3))
        return 0

    lax.fori_loop(0, last + 1, tick, 0)

    m_partial(1)
    weight_grads(experts - 1)
    m_step(0, 4)
    m_step(1, 2)
    m_end(0)
    m_step(1, 3)
    m_final(0, mixed_out)
    m_step(1, 4)
    m_end(1)

    for n, ref in enumerate((
        PSa, PSb, Y1a.at[:, 0], Y1a.at[:, 1], Y2a.at[:, 0], Y2a.at[:, 1], XSa, Xb,
        Y1b.at[:, 0], Y1b.at[:, 1], Y2b.at[:, 0], Y2b.at[:, 1],
    )):
        sent(ref, rs_s.at[n])
    for m in range(14):
        if m < 7:
            ref = Fa.at[:, c, y, xh]
        elif m < 9:
            ref = Fb.at[:, c, y, xh]
        elif m < 11:
            ref = Fb.at[:, c, y, xh, 0]
        elif m == 11:
            ref = Fb.at[:, c, :, xh]
        else:
            ref = (Fa if m == 12 else Fb).at[:, c]
        sent(ref, ag_s.at[m])
    tk_drain(0)
    tk_drain(1)
    m_final(1, gt_out)
    m_drain(0)
    m_drain(1)


def copy_out(mixed, grad_tokens, grads, mixed_out, gt_out, gg_out, gu_out, gd_out, sem):
    copies = [
        pltpu.make_async_copy(mixed, mixed_out, sem.at[0]),
        pltpu.make_async_copy(grad_tokens, gt_out, sem.at[1]),
    ]
    for i, out in enumerate((gg_out, gu_out, gd_out)):
        for e in range(out.shape[0]):
            for h in range(2):
                rows = pl.ds(h * (out.shape[1] // 2), out.shape[1] // 2)
                copies.append(pltpu.make_async_copy(grads.at[i, e, rows], out.at[e, rows], sem.at[len(copies)]))
    for cp in copies:
        cp.start()
    for cp in copies:
        cp.wait()


def body(tokens, routes, combine, w_gate, w_up, w_down, cotangent):
    experts, width, hidden = w_gate.shape
    half = hidden // 2
    total = routes.shape[0]
    block = tokens.shape[0]
    items = 3 * experts
    vm = pl.BlockSpec(memory_space=pltpu.VMEM)
    hbm = pl.BlockSpec(memory_space=pl.ANY)
    V = pltpu.VMEM
    DMA = pltpu.SemaphoreType.DMA
    scratch = [
        V((3, 2, experts, width, half), BF),
        V((2, 2, 8, 2, width // 2, block), BF),
        V((experts, CP, total), BF),
        V((experts, CP, 128), F32),
        V((experts, 128, CP), F32),
        V((2, experts, CP, width), BF),
        V((2, experts, width, CP), BF),
        V((items, 4, 2, ROWS, WA), BF),
        V((items, 4, 2, 2, ROWS, WB), BF),
        V((items, 4, 2, ROWS, WA), BF),
        V((items, 4, 2, 2, ROWS, WB), BF),
        V((items, 4, 2, ROWS, WA), BF),
        V((items, 4, 2, 2, ROWS, WB), BF),
        V((items, 2, ROWS, WA), BF),
        V((items, 2, 2, ROWS, WA), BF),
        V((items, ROWS, WA), BF),
        V((items, ROWS, WA), BF),
        V((items, 4, 2, ROWS, WB), BF),
        V((items, 2, ROWS, WB), BF),
        V((items, 2, 2, ROWS, WB), BF),
        V((2, experts, ROWS, WA), F32),
        V((2, experts, 2, ROWS, WB), F32),
        V((items, 2, 4, 2, ROWS, WA), BF),
        V((items, 2, 4, 2, 2, ROWS, WB), BF),
        V((2, experts, width, CP), BF),
        V((2, 2, 8, 2, width // 2, block), BF),
        V((2, 2, 4, 2, 2, width // 2, block), BF),
        V((2, 2, width // 2, block), BF),
        V((2, 2, width // 2, block), BF),
        V((CP, 256), F32),
        DMA((6,)),
        DMA((12,)),
        DMA((items, 11)),
        DMA((14,)),
        DMA((items, 8)),
        DMA((2, 3)),
        DMA((2, 34)),
        DMA((2, 3)),
        DMA((2, 34)),
    ]
    small = jax.ShapeDtypeStruct((width, block), BF)
    large = jax.ShapeDtypeStruct(w_gate.shape, BF)
    call = pl.pallas_call(
        kernel,
        out_shape=(V((width, block), BF), V((width, block), BF), V((3, experts, width, hidden), BF)),
        in_specs=[vm, vm, vm, vm, hbm, hbm, hbm],
        out_specs=(vm, vm, vm),
        scratch_shapes=scratch,
        compiler_params=pltpu.CompilerParams(
            collective_id=0, has_side_effects=True, vmem_limit_bytes=55 * 2**20
        ),
    )
    results = call(
        tokens.T, cotangent.T, routes.T, combine.T, w_gate, w_up, jnp.swapaxes(w_down, 1, 2)
    )
    mixed, grad_tokens, grad_gate, grad_up, grad_down = pl.pallas_call(
        copy_out,
        out_shape=(small, small, large, large, large),
        in_specs=[vm] * 3,
        out_specs=(hbm,) * 5,
        scratch_shapes=[DMA((2 + 6 * experts,))],
        compiler_params=pltpu.CompilerParams(vmem_limit_bytes=2**20),
    )(*(pltpu.with_memory_space_constraint(r, pltpu.VMEM) for r in results))
    return mixed.T, grad_tokens.T, grad_gate, grad_up, jnp.swapaxes(grad_down, 1, 2)


def solution(mesh):
    rows = P("expert", "dp")
    wide = P("expert", "dp", None)
    deep = P("expert", None, "dp")
    return jax.shard_map(
        body,
        mesh=mesh,
        in_specs=(rows, P(), P(), wide, wide, deep, rows),
        out_specs=(rows, rows, wide, wide, deep),
        check_vma=False,
    )
```

```python
import jax
import jax.numpy as jnp
from jax import lax
from jax.experimental import pallas as pl
from jax.experimental.pallas import tpu as pltpu
from jax.sharding import PartitionSpec as P

MESH = pl.DeviceIdType.MESH
BF = jnp.bfloat16
F32 = jnp.float32

SUM_AT = (0, 2, 3, 4, 5)
GATHER_AT = (0, 1, 2, 3, 4)
CP = 384
ROWS = 48
WA = 384
WB = 128


def dot(a, b):
    return jnp.dot(a, b, preferred_element_type=F32)


def dot_nt(a, b):
    return lax.dot_general(a, b, (((1,), (1,)), ((), ())), preferred_element_type=F32)


def kernel(
    tok, cot, routes, combine, wg, wu, wd,
    mixed_out, gt_out, GS,
    W, TK, A, WT, WR, PK, PT, PSa, PSb, Qa, Qb, CRa, CRb,
    Y1a, Y2a, Xa, XSa, Xb, Y1b, Y2b, GUa, GUb, Fa, Fb,
    YT, MP, MR, MX, MXS, TP,
    wsem, rs_s, rs_r, ag_s, ag_r, tk_s, tk_r, m_s, m_r,
):
    experts, width = wg.shape[0], wg.shape[1]
    half = wg.shape[2] // 2
    tokens = routes.shape[1]
    d = lax.axis_index("dp")
    ex = lax.axis_index("expert")
    y, xh, c = d // 4, (d // 2) % 2, d % 2
    xl, z = ex // 8, ex % 8
    yr, yl, yo = (y + 1) % 4, (y + 3) % 4, (y + 2) % 4
    xo, co, xlo = 1 - xh, 1 - c, 1 - xl

    def dev(yy, xx, cc, ll, zz):
        return (yy * 4 + xx * 2 + cc, ll * 8 + zz)

    CORE = dev(y, xh, co, xl, z)
    YR = dev(yr, xh, c, xl, z)
    YL = dev(yl, xh, c, xl, z)
    XH = dev(y, xo, c, xl, z)
    XL = dev(y, xh, c, xlo, z)
    ZR = dev(y, xh, c, xl, (z + 1) % 8)
    ZL = dev(y, xh, c, xl, (z + 7) % 8)

    def remote(src, dst, ss, rr, to):
        return pltpu.make_async_remote_copy(
            src_ref=src, dst_ref=dst, send_sem=ss, recv_sem=rr,
            device_id=to, device_id_type=MESH,
        )

    def came(ref, sem):
        remote(ref, ref, sem, sem, CORE).wait_recv()

    def sent(ref, sem):
        remote(ref, ref, sem, sem, CORE).wait_send()

    def weight_copies():
        out = []
        for i, w in enumerate((wg, wu, wd)):
            for h in range(2):
                out.append(pltpu.make_async_copy(
                    w.at[:, :, pl.ds(h * half, half)], W.at[i, h], wsem.at[i * 2 + h]))
        return out

    barrier = pltpu.get_barrier_semaphore()
    for peer in (CORE, YR, YL, XH, XL, ZR, ZL):
        pl.semaphore_signal(barrier, inc=1, device_id=peer, device_id_type=MESH)
    for cp in weight_copies():
        cp.start()

    for i, src in enumerate((tok, cot)):
        for f in range(2):
            TK[i, xl, z, f] = src[f * (width // 2):(f + 1) * (width // 2)]
    pl.semaphore_wait(barrier, 7)

    def tk_x(i, f):
        r = TK.at[i, xl, z, f]
        return remote(r, r, tk_s.at[i, 2], tk_r.at[i, 32 + f], XL)

    def tk_z(i, way, s, b, f):
        zs = (z + 8 - (s - 1)) % 8 if way == 0 else (z + (s - 1)) % 8
        r = TK.at[i, b, zs, f]
        n = ((way * 4 + s - 1) * 2 + b) * 2 + f
        return remote(r, r, tk_s.at[i, way], tk_r.at[i, n], ZR if way == 0 else ZL)

    def tk0(i):
        for f in range(2):
            for way in (0, 1):
                tk_z(i, way, 1, xl, f).start()
            tk_x(i, f).start()

    def tk1(i):
        for f in range(2):
            tk_x(i, f).wait_recv()
            for way in (0, 1):
                tk_z(i, way, 1, xlo, f).start()

    def tk_hop(i, s):
        if s < 3:
            for b in (xl, xlo):
                for f in range(2):
                    for way in (0, 1):
                        tk_z(i, way, s, b, f).wait_recv()
                        tk_z(i, way, s + 1, b, f).start()
        elif s == 3:
            for f in range(2):
                for way in (0, 1):
                    tk_z(i, way, 3, way, f).wait_recv()
                    tk_z(i, way, 4, way, f).start()
            for f in range(2):
                for way in (0, 1):
                    tk_z(i, way, 3, 1 - way, f).wait_recv()
        else:
            for f in range(2):
                for way in (0, 1):
                    tk_z(i, way, 4, way, f).wait_recv()

    def tk_drain(i):
        sent(TK.at[i, 0, 0], tk_s.at[i, 2])
        for way in (0, 1):
            sent(TK.at[i, 0, pl.ds(0, 7)], tk_s.at[i, way])

    def token_rows(i):
        return jnp.concatenate([TK[i, n // 8, n % 8].reshape(width, 128) for n in range(16)], axis=1)

    def m_dest(way, s):
        return (z + 5 - s) % 8 if way == 0 else (z + 3 + s) % 8

    def m_z(i, way, s, b, f):
        n = ((way * 4 + s - 1) * 2 + b) * 2 + f
        return remote(
            MP.at[i, b, m_dest(way, s), f], MR.at[i, way, s - 1, b, f],
            m_s.at[i, way], m_r.at[i, n], ZR if way == 0 else ZL)

    def m_x(i, f):
        return remote(MXS.at[i, f], MX.at[i, f], m_s.at[i, 2], m_r.at[i, 32 + f], XL)

    def m_partial(i):
        for q in (2, 0, 3, 1):
            acc = dot(YT[i, 0], A[0, :, q * 512:(q + 1) * 512])
            for e in range(1, experts):
                acc = acc + dot(YT[i, e], A[e, :, q * 512:(q + 1) * 512])
            acc = acc.astype(BF)
            for j in range(4):
                n = q * 4 + j
                MP[i, n // 8, n % 8] = acc[:, j * 128:(j + 1) * 128].reshape(2, width // 2, 128)
        for f in range(2):
            for way in (0, 1):
                m_z(i, way, 1, way, f).start()
        for f in range(2):
            for way in (0, 1):
                m_z(i, way, 2, 1 - way, f).start()

    def m_add(i, way, s, b, f):
        m_z(i, way, s - 1, b, f).wait_recv()
        zd = m_dest(way, s)
        MP[i, b, zd, f] = (MP[i, b, zd, f].astype(F32) + MR[i, way, s - 2, b, f].astype(F32)).astype(BF)
        m_z(i, way, s, b, f).start()

    def m_step(i, s):
        for n in range(1 if s == 2 else 2):
            for f in range(2):
                for way in (0, 1):
                    m_add(i, way, s, way if n == 0 else 1 - way, f)

    def m_sum(i, b, f):
        m_z(i, 0, 4, b, f).wait_recv()
        m_z(i, 1, 4, b, f).wait_recv()
        return MP[i, b, z, f].astype(F32) + MR[i, 0, 3, b, f].astype(F32) + MR[i, 1, 3, b, f].astype(F32)

    def m_end(i):
        for f in range(2):
            MXS[i, f] = m_sum(i, xlo, f).astype(BF)
            m_x(i, f).start()

    def m_final(i, out):
        for f in range(2):
            own = m_sum(i, xl, f)
            m_x(i, f).wait_recv()
            out[f * (width // 2):(f + 1) * (width // 2)] = (own + MX[i, f].astype(F32)).astype(BF)

    def m_drain(i):
        for way in (0, 1):
            sent(MP.at[i, 0, pl.ds(0, 7)], m_s.at[i, way])
        sent(MXS.at[i], m_s.at[i, 2])

    def rs(k, n):
        s, r = rs_s.at[n], rs_r.at[k, {5: 4, 11: 10}.get(n, n)]
        if n == 0:
            return remote(PSa.at[k], CRa.at[k], s, r, CORE)
        if n == 1:
            return remote(PSb.at[k], CRb.at[k], s, r, CORE)
        if n == 2:
            return remote(Qa.at[k, yo, 0], Y1a.at[k, 0], s, r, YR)
        if n == 3:
            return remote(Qa.at[k, yo, 1], Y1a.at[k, 1], s, r, YL)
        if n == 4:
            return remote(Qa.at[k, yr], Y2a.at[k, 0], s, r, YR)
        if n == 5:
            return remote(Qa.at[k, yl], Y2a.at[k, 1], s, r, YL)
        if n == 6:
            return remote(XSa.at[k], Xa.at[k], s, r, XH)
        if n == 7:
            return remote(Qb.at[k, :, xo], Xb.at[k], s, r, XH)
        if n == 8:
            return remote(Qb.at[k, yo, xh, 0], Y1b.at[k, 0], s, r, YR)
        if n == 9:
            return remote(Qb.at[k, yo, xh, 1], Y1b.at[k, 1], s, r, YL)
        if n == 10:
            return remote(Qb.at[k, yr, xh], Y2b.at[k, 0], s, r, YR)
        return remote(Qb.at[k, yl, xh], Y2b.at[k, 1], s, r, YL)

    def put(ra, rb, k, v):
        v = v.astype(BF)
        ra[k] = v[:, :WA].reshape(4, 2, ROWS, WA)
        for p in range(2):
            rb[k, :, :, p] = v[:, WA + p * WB:WA + (p + 1) * WB].reshape(4, 2, ROWS, WB)

    def s0(k, part):
        put(PSa, PSb, k, part(co))
        rs(k, 0).start()
        rs(k, 1).start()
        put(Qa, Qb, k, part(c))

    def add(ref, idx, other):
        ref[idx] = (ref[idx].astype(F32) + other.astype(F32)).astype(BF)

    def s1(k):
        rs(k, 0).wait_recv()
        add(Qa, (k, yo), CRa[k, yo])
        rs(k, 2).start()
        rs(k, 3).start()
        rs(k, 1).wait_recv()
        for j in range(4):
            add(Qb, (k, j), CRb[k, j])
        rs(k, 7).start()
        for j in (yr, yl, y):
            add(Qa, (k, j), CRa[k, j])

    def s2(k):
        rs(k, 2).wait_recv()
        add(Qa, (k, yr, 0), Y1a[k, 0])
        rs(k, 4).start()
        rs(k, 3).wait_recv()
        add(Qa, (k, yl, 1), Y1a[k, 1])
        rs(k, 5).start()
        rs(k, 7).wait_recv()
        add(Qb, (k, yo, xh), Xb[k, yo])
        rs(k, 8).start()
        rs(k, 9).start()
        for j in (yr, yl, y):
            add(Qb, (k, j, xh), Xb[k, j])

    def sum_a(k, x):
        return Qa[k, y, x].astype(F32) + Y2a[k, 0, x].astype(F32) + Y2a[k, 1, x].astype(F32)

    def s3(k):
        rs(k, 8).wait_recv()
        add(Qb, (k, yr, xh, 0), Y1b[k, 0])
        rs(k, 10).start()
        rs(k, 9).wait_recv()
        add(Qb, (k, yl, xh, 1), Y1b[k, 1])
        rs(k, 11).start()
        came(Y2a.at[k], rs_r.at[k, 4])
        XSa[k] = sum_a(k, xo).astype(BF)
        rs(k, 6).start()

    def s4(k):
        rs(k, 6).wait_recv()
        va = sum_a(k, xh) + Xa[k].astype(F32)
        came(Y2b.at[k], rs_r.at[k, 10])
        vb = Qb[k, y, xh].astype(F32) + Y2b[k, 0].astype(F32) + Y2b[k, 1].astype(F32)
        return va, vb

    def hidden_of(gate, up):
        return (gate * jax.nn.sigmoid(gate) * up).astype(BF)

    def grads_of(back, gate, up):
        sg = jax.nn.sigmoid(gate)
        return (back * up * sg * (1.0 + gate * (1.0 - sg))).astype(BF), (back * gate * sg).astype(BF)

    def ag(g, j, n, m):
        s, r = ag_s.at[m], ag_r.at[g, (0, 1, 1, 1, 1, 2, 2, 3, 3, 4, 4, 5, 6, 7)[m]]
        js = pl.ds(j, n)
        if m == 0:
            ref, to = Fa.at[js, c, y, xh], XH
        elif m in (1, 2):
            ref, to = Fa.at[js, c, y, xh], (YR if m == 1 else YL)
        elif m in (3, 4):
            ref, to = Fa.at[js, c, y, xo], (YR if m == 3 else YL)
        elif m == 5:
            ref, to = Fa.at[js, c, yl, 0], YR
        elif m == 6:
            ref, to = Fa.at[js, c, yr, 1], YL
        elif m in (7, 8):
            ref, to = Fb.at[js, c, y, xh], (YR if m == 7 else YL)
        elif m == 9:
            ref, to = Fb.at[js, c, yl, xh, 0], YR
        elif m == 10:
            ref, to = Fb.at[js, c, yr, xh, 1], YL
        elif m == 11:
            ref, to = Fb.at[js, c, :, xh], XH
        elif m == 12:
            ref, to = Fa.at[js, c], CORE
        else:
            ref, to = Fb.at[js, c], CORE
        return remote(ref, ref, s, r, to)

    def ag_stage(i, g, j, n):
        js = pl.ds(j, n)
        if i == 0:
            for m in (0, 1, 2, 7, 8):
                ag(g, j, n, m).start()
        if i == 1:
            ag(g, j, n, 0).wait_recv()
            ag(g, j, n, 3).start()
            ag(g, j, n, 4).start()
            came(Fb.at[js, c, 0], ag_r.at[g, 3])
            ag(g, j, n, 9).start()
            ag(g, j, n, 10).start()
        if i == 2:
            came(Fa.at[js, c, pl.ds(0, 2)], ag_r.at[g, 1])
            ag(g, j, n, 5).start()
            ag(g, j, n, 6).start()
            came(Fb.at[js, c, 0, 0], ag_r.at[g, 4])
            ag(g, j, n, 11).start()
        if i == 3:
            came(Fa.at[js, c, 0], ag_r.at[g, 2])
            ag(g, j, n, 12).start()
            ag(g, j, n, 11).wait_recv()
            ag(g, j, n, 13).start()
        if i == 4:
            ag(g, j, n, 12).wait_recv()
            ag(g, j, n, 13).wait_recv()

    def full(j, h):
        return jnp.concatenate(
            [Fa[j, h].reshape(CP, WA), Fb[j, h, :, :, 0].reshape(CP, WB), Fb[j, h, :, :, 1].reshape(CP, WB)], axis=1)

    def turn(v):
        TP[:, :width] = v
        return jnp.transpose(TP[...])[:width].astype(BF)

    def use_hidden(e):
        acc = jnp.zeros((width, CP), F32)
        for h in range(2):
            f = full(e, h)
            acc = acc + dot_nt(W[2, h, e], f)
            GS[2, e, :, h * half:(h + 1) * half] = dot(PT[1, e], f).astype(BF)
        YT[0, e] = (acc * WR[e, 0:1]).astype(BF)

    def use_grads(e):
        acc = jnp.zeros((width, CP), F32)
        for i in range(2):
            for h in range(2):
                acc = acc + dot_nt(W[i, h, e], full(experts + 2 * e + i, h))
        YT[1, e] = acc.astype(BF)

    def weight_grads(e):
        for i in range(2):
            for h in range(2):
                f = full(experts + 2 * e + i, h)
                GS[i, e, :, h * half:(h + 1) * half] = dot(PT[0, e], f).astype(BF)

    tk0(0)
    TP[...] = jnp.zeros_like(TP)
    lane = lax.broadcasted_iota(jnp.int32, (1, tokens), 1)
    for e in range(experts):
        same = routes[...] == ex * experts + e
        routed = jnp.max(jnp.where(same, 1, 0), axis=0, keepdims=True)
        weight = jnp.sum(jnp.where(same, combine[...], 0.0), axis=0, keepdims=True)
        rank = jnp.broadcast_to(routed, (8, tokens))
        lanes = jnp.broadcast_to(lane, (8, tokens))
        step = 1
        while step < tokens:
            rank = rank + jnp.where(lanes >= step, pltpu.roll(rank, step, 1), 0)
            step *= 2
        pos = jnp.where(routed > 0, rank[0:1] - 1, -1)
        if e == 0:
            tk1(0)

        def fill(i, _, e=e, pos=pos, weight=weight):
            at = pl.ds(pl.multiple_of(i * 32, 32), 32)
            hit = lax.broadcasted_iota(jnp.int32, (32, tokens), 0) + i * 32 == pos
            A[e, at] = jnp.where(hit, 1.0, 0.0).astype(BF)
            WT[e, at] = jnp.broadcast_to(
                jnp.sum(jnp.where(hit, weight, 0.0), axis=1, keepdims=True), (32, 128))
            return 0

        lax.fori_loop(0, CP // 32, fill, 0)
        WR[e] = jnp.transpose(WT[e])
        tk_hop(0, e + 1)
    tk_hop(0, 4)
    for cp in weight_copies():
        cp.wait()

    def pick(e):
        v = dot_nt(A[e], token_rows(0))
        PK[0, e] = v.astype(BF)
        PT[0, e] = turn(v)

    pick(0)

    gu = 2 * experts
    items = gu + experts
    ag_h = 1 + SUM_AT[4]
    ag_p = gu + SUM_AT[4]
    last = ag_p + experts - 1 + GATHER_AT[4]

    def tick(t, _):
        def at(k, lo, hi, f):
            @pl.when(jnp.logical_and(k >= lo, k < hi))
            def _():
                f(k)

        def on(k, f):
            @pl.when(t == k)
            def _():
                f()

        at(t, 0, gu, lambda k: s0(k, lambda h: dot(PK[0, k // 2], W[k % 2, h, k // 2])))
        at(t, gu, items, lambda k: s0(k, lambda h: dot(PK[1, k - gu], W[2, h, k - gu])))
        at(t - SUM_AT[1], 0, items, s1)
        at(t - SUM_AT[2], 0, items, s2)
        at(t - SUM_AT[3], 0, items, s3)

        def end(k):
            va, vb = s4(k)

            @pl.when(k < gu)
            def _():
                GUa[k % 2, k // 2] = va
                GUb[k % 2, k // 2] = vb

            @pl.when(jnp.logical_and(k < gu, k % 2 == 1))
            def _():
                e = k // 2
                Fa[e, c, y, xh] = hidden_of(GUa[0, e], va)
                Fb[e, c, y, xh] = hidden_of(GUb[0, e], vb)
                ag_stage(0, e, e, 1)

            @pl.when(k >= gu)
            def _():
                e = k - gu
                j = experts + 2 * e
                Fa[j, c, y, xh], Fa[j + 1, c, y, xh] = grads_of(va, GUa[0, e], GUa[1, e])
                Fb[j, c, y, xh], Fb[j + 1, c, y, xh] = grads_of(vb, GUb[0, e], GUb[1, e])
                ag_stage(0, j, j, 1)
                ag_stage(0, j + 1, j + 1, 1)

        at(t - SUM_AT[4], 0, items, end)

        for i in range(1, 5):
            u = t - ag_h - GATHER_AT[i]

            @pl.when(jnp.logical_and(jnp.logical_and(u >= 0, u < 2 * experts), u % 2 == 0))
            def _(u=u, i=i):
                e = u // 2
                ag_stage(i, e, e, 1)
                if i == 4:
                    use_hidden(e)

            def grads_stage(e, i=i):
                ag_stage(i, experts + 2 * e, experts + 2 * e, 1)
                ag_stage(i, experts + 2 * e + 1, experts + 2 * e + 1, 1)
                if i == 4:
                    use_grads(e)

                    @pl.when(e < experts - 1)
                    def _():
                        weight_grads(e)

            at(t - ag_p - GATHER_AT[i], 0, experts, grads_stage)

        for e in range(1, experts):
            on(e - 1, lambda e=e: pick(e))
        on(0, lambda: tk0(1))
        on(1, lambda: tk1(1))
        on(2, lambda: tk_hop(1, 1))
        on(3, lambda: tk_hop(1, 2))
        on(4, lambda: tk_hop(1, 3))

        def cot_slots():
            tk_hop(1, 4)
            crow = token_rows(1)
            for e in range(experts):
                v = dot_nt(A[e], crow) * WT[e, :, 0:1]
                PK[1, e] = v.astype(BF)
                PT[1, e] = turn(v)

        on(gu - 1, cot_slots)
        m0 = ag_h + 2 * (experts - 1) + GATHER_AT[4]
        on(m0, lambda: m_partial(0))
        on(m0 + 1, lambda: m_step(0, 2))
        on(m0 + 2, lambda: m_step(0, 3))
        return 0

    lax.fori_loop(0, last + 1, tick, 0)

    m_partial(1)
    weight_grads(experts - 1)
    m_step(0, 4)
    m_step(1, 2)
    m_end(0)
    m_step(1, 3)
    m_final(0, mixed_out)
    m_step(1, 4)
    m_end(1)

    for n, ref in enumerate((
        PSa, PSb, Y1a.at[:, 0], Y1a.at[:, 1], Y2a.at[:, 0], Y2a.at[:, 1], XSa, Xb,
        Y1b.at[:, 0], Y1b.at[:, 1], Y2b.at[:, 0], Y2b.at[:, 1],
    )):
        sent(ref, rs_s.at[n])
    for m in range(14):
        if m < 7:
            ref = Fa.at[:, c, y, xh]
        elif m < 9:
            ref = Fb.at[:, c, y, xh]
        elif m < 11:
            ref = Fb.at[:, c, y, xh, 0]
        elif m == 11:
            ref = Fb.at[:, c, :, xh]
        else:
            ref = (Fa if m == 12 else Fb).at[:, c]
        sent(ref, ag_s.at[m])
    tk_drain(0)
    tk_drain(1)
    m_final(1, gt_out)
    m_drain(0)
    m_drain(1)


def copy_out(mixed, grad_tokens, grads, mixed_out, gt_out, gg_out, gu_out, gd_out, sem):
    copies = [
        pltpu.make_async_copy(mixed, mixed_out, sem.at[0]),
        pltpu.make_async_copy(grad_tokens, gt_out, sem.at[1]),
    ]
    for i, out in enumerate((gg_out, gu_out, gd_out)):
        for e in range(out.shape[0]):
            for h in range(2):
                rows = pl.ds(h * (out.shape[1] // 2), out.shape[1] // 2)
                copies.append(pltpu.make_async_copy(grads.at[i, e, rows], out.at[e, rows], sem.at[len(copies)]))
    for cp in copies:
        cp.start()
    for cp in copies:
        cp.wait()


def body(tokens, routes, combine, w_gate, w_up, w_down, cotangent):
    experts, width, hidden = w_gate.shape
    half = hidden // 2
    total = routes.shape[0]
    block = tokens.shape[0]
    items = 3 * experts
    vm = pl.BlockSpec(memory_space=pltpu.VMEM)
    hbm = pl.BlockSpec(memory_space=pl.ANY)
    V = pltpu.VMEM
    DMA = pltpu.SemaphoreType.DMA
    scratch = [
        V((3, 2, experts, width, half), BF),
        V((2, 2, 8, 2, width // 2, block), BF),
        V((experts, CP, total), BF),
        V((experts, CP, 128), F32),
        V((experts, 128, CP), F32),
        V((2, experts, CP, width), BF),
        V((2, experts, width, CP), BF),
        V((items, 4, 2, ROWS, WA), BF),
        V((items, 4, 2, 2, ROWS, WB), BF),
        V((items, 4, 2, ROWS, WA), BF),
        V((items, 4, 2, 2, ROWS, WB), BF),
        V((items, 4, 2, ROWS, WA), BF),
        V((items, 4, 2, 2, ROWS, WB), BF),
        V((items, 2, ROWS, WA), BF),
        V((items, 2, 2, ROWS, WA), BF),
        V((items, ROWS, WA), BF),
        V((items, ROWS, WA), BF),
        V((items, 4, 2, ROWS, WB), BF),
        V((items, 2, ROWS, WB), BF),
        V((items, 2, 2, ROWS, WB), BF),
        V((2, experts, ROWS, WA), F32),
        V((2, experts, 2, ROWS, WB), F32),
        V((items, 2, 4, 2, ROWS, WA), BF),
        V((items, 2, 4, 2, 2, ROWS, WB), BF),
        V((2, experts, width, CP), BF),
        V((2, 2, 8, 2, width // 2, block), BF),
        V((2, 2, 4, 2, 2, width // 2, block), BF),
        V((2, 2, width // 2, block), BF),
        V((2, 2, width // 2, block), BF),
        V((CP, 256), F32),
        DMA((6,)),
        DMA((12,)),
        DMA((items, 11)),
        DMA((14,)),
        DMA((items, 8)),
        DMA((2, 3)),
        DMA((2, 34)),
        DMA((2, 3)),
        DMA((2, 34)),
    ]
    small = jax.ShapeDtypeStruct((width, block), BF)
    large = jax.ShapeDtypeStruct(w_gate.shape, BF)
    call = pl.pallas_call(
        kernel,
        out_shape=(V((width, block), BF), V((width, block), BF), V((3, experts, width, hidden), BF)),
        in_specs=[vm, vm, vm, vm, hbm, hbm, hbm],
        out_specs=(vm, vm, vm),
        scratch_shapes=scratch,
        compiler_params=pltpu.CompilerParams(
            collective_id=0, has_side_effects=True, vmem_limit_bytes=55 * 2**20
        ),
    )
    results = call(
        tokens.T, cotangent.T, routes.T, combine.T, w_gate, w_up, jnp.swapaxes(w_down, 1, 2)
    )
    mixed, grad_tokens, grad_gate, grad_up, grad_down = pl.pallas_call(
        copy_out,
        out_shape=(small, small, large, large, large),
        in_specs=[vm] * 3,
        out_specs=(hbm,) * 5,
        scratch_shapes=[DMA((2 + 6 * experts,))],
        compiler_params=pltpu.CompilerParams(vmem_limit_bytes=2**20),
    )(*(pltpu.with_memory_space_constraint(r, pltpu.VMEM) for r in results))
    return mixed.T, grad_tokens.T, grad_gate, grad_up, jnp.swapaxes(grad_down, 1, 2)


def solution(mesh):
    rows = P("expert", "dp")
    wide = P("expert", "dp", None)
    deep = P("expert", None, "dp")
    return jax.shard_map(
        body,
        mesh=mesh,
        in_specs=(rows, P(), P(), wide, wide, deep, rows),
        out_specs=(rows, rows, wide, wide, deep),
        check_vma=False,
    )
```
